32 devices in a mesh: replica: 4 (over y, x), shard: 8 (over z, core).
Axes of the slice: x: 2, y: 2, z: 4, core: 2. Of those that a mesh axis runs over, the one named last changes fastest.
Arguments:
- table: float32 [2048, 1024], P('shard'), may hold values from -6 to 6
- accum: float32 [2048], P('shard'), may hold values from 0.0001 to 0.01
- owner: int32 [8192, 1], P(('replica', 'shard')), may hold values from 0 to 7; in each aligned block of 256 rows (0 to 255, 256 to 511, ...) at most 64 rows name the same one
- local_row: int32 [8192], P(('replica', 'shard')), may hold values from 0 to 255
- lengths: int32 [32, 4], P(('replica', 'shard')), may hold values from 1 to 128, 256 in all within a row
- queries: bfloat16 [8192, 512], P(('replica', 'shard')), may hold values from -6 to 6
- keys: bfloat16 [8192, 512], P(('replica', 'shard')), may hold values from -6 to 6
- cotangent: bfloat16 [8192, 1024], P(('replica', 'shard')), may hold values from -6 to 6
- out_weight: bfloat16 [1024, 1024], P('shard'), may hold values from -0.1875 to 0.1875
Outputs:
- new_table: float32 [2048, 1024], P('shard')
- new_accum: float32 [2048], P('shard')
- weight_grad: bfloat16 [1024, 1024], P('shard')
The draws below stay inside these ranges and needn't reach their ends.
Inputs may be any that keep to these rules, and one draw needn't show every extreme that they name: Among the 256 tokens of one device no owner is named more than 64 times; in every draw some owner is named exactly 64 times by some device's tokens. Each row holds positive lengths that sum to 256; the largest of each row is 128.
All inputs are finite; a program needn't handle non-finite values.
Results may differ from the reference program's by a relative error of at most 0.0064.
Values may be sent and summed in bfloat16 or wider, within the bound.
No kernel may reach another device: no remote copies, remote signals or barrier semaphores. Data moves between devices by JAX's collectives and lax.ppermute only.
A program may use at most 64 MiB of HBM per device.

```python
import math
import jax
import jax.numpy as jnp
import numpy as np
from jax import lax

D = 1024
HEADS = 8
DQK = 64
DOUT = 1024
TOK_DEV = 256
ROWS_DEV = 256
MAXLEN = 128
DV = 128
CAP = 64
NSEQ = 4
TOKENS = 8192
ROWS = 2048
N_REPLICA = 4
N_SHARD = 8


def set_ends(values, key, least, largest):
    longest = values.shape.index(max(values.shape))
    spots = []
    for shift in (0, 1):
        where = [jax.random.randint(jax.random.fold_in(key, axis), (), 0, length) for axis, length in enumerate(values.shape)]
        where[longest] = (where[longest] + shift) % values.shape[longest]
        spots.append(tuple(where))
    return values.at[spots[0]].set(least).at[spots[1]].set(largest)


def block_scale(key, dims, cuts, low, largest):
    def one(dim, blocks):
        draws = jax.random.uniform(jax.random.fold_in(jax.random.fold_in(key, 6), dim), (blocks,), jnp.float32, low / len(cuts), largest / len(cuts))
        return jnp.repeat(jnp.exp(draws), dims[dim] // blocks).reshape((-1,) + (1,) * (len(dims) - dim - 1))

    gain = one(*cuts[0])
    for cut in cuts[1:]:
        gain = gain * one(*cut)
    return gain


def length_profile(number_of, total, most, skew):
    weights = [(1 << 20) // math.isqrt(grade ** skew) + 1 for grade in range(2, number_of + 1)]
    surplus, holding = total - most - (number_of - 1), [1] * (number_of - 1)
    while surplus > 0:
        movable = [i for i in range(number_of - 1) if holding[i] < most]
        pool, budget = sum([weights[i] for i in movable]), surplus
        for i in movable:
            extra = min(most - holding[i], max(1, budget * weights[i] // pool), surplus)
            holding[i] = holding[i] + extra
            surplus = surplus - extra
    return np.array([most] + holding)


def uneven_parts(own_key, count, total, limit, skew):
    if count == 2:
        one = jax.random.randint(own_key, (), max(1, total - limit), min(limit, total - 1) + 1)
        return jnp.stack([one, total - one])
    tallies = jnp.asarray(length_profile(count, total, limit, skew), jnp.int32)
    pairs = (count - 1) // 2
    source_of, sink = tallies[1:1 + 2 * pairs:2], tallies[2:2 + 2 * pairs:2]
    slack = jnp.minimum(source_of - 1, limit - sink)
    shifted = jax.random.randint(jax.random.fold_in(own_key, 1), (pairs,), 0, 1 << 20) % (slack + 1)
    tallies = tallies.at[1:1 + 2 * pairs:2].set(source_of - shifted).at[2:2 + 2 * pairs:2].set(sink + shifted)
    return tallies[jax.random.permutation(jax.random.fold_in(own_key, 2), count)]


def routed_block(rng, own, number, rows, count, top, most, slope):
    order = jax.random.permutation(rng, count)
    crowded, usual = portions_of(count, rows * top, most, slope, True), portions_of(count, rows * top, most, slope, False)
    places = jnp.arange(count)

    def named(tallies, offset_by):
        used = int((tallies > 0).sum())
        fixed = max(1, used // 4)
        shifted = fixed + (places - fixed + offset_by * (used - fixed)) % max(1, count - fixed)
        return jnp.zeros((count,), jnp.int32).at[order[jnp.where(places < fixed, places, shifted)]].set(jnp.asarray(tallies, jnp.int32))

    tallies = jnp.where(number % 4 == 0, named(crowded, number // 4), named(usual, number - number // 4 - 1))
    mixed = jax.random.permutation(jax.random.fold_in(own, 3), count)
    source_of, sink = mixed[0:count // 2 * 2:2], mixed[1:count // 2 * 2:2]
    room = jnp.minimum(tallies[source_of] - 1, most - tallies[sink]) // 2
    room = jnp.where((source_of == order[0]) | (sink == order[0]) | (tallies[sink] == 0), 0, jnp.maximum(room, 0))
    shifted = jax.random.randint(jax.random.fold_in(own, 4), (count // 2,), 0, 1 << 20) % (room + 1)
    tallies = tallies.at[source_of].add(-shifted).at[sink].add(shifted)
    labels = jnp.searchsorted(jnp.cumsum(tallies), jnp.arange(rows * top), side="right").astype(jnp.int32)
    grid = labels.reshape(top, rows).T
    grid = grid[jax.random.permutation(jax.random.fold_in(own, 1), rows)]
    offset_by = jax.random.randint(jax.random.fold_in(own, 2), (rows, 1), 0, top)
    return jnp.take_along_axis(grid, (jnp.arange(top)[None, :] + offset_by) % top, axis=1)


def portions_of(amount, total, bound, slope, full):
    loads = [(1 << 20) // math.isqrt(standing ** slope) + 1 for standing in range(1, amount + 1)]
    largest = bound if full else min(bound, max(-(-total // amount), total * loads[0] // sum(loads)))
    least = 1 if total - largest >= amount - 1 else 0
    given, spare = [largest] + [least] * (amount - 1), total - largest - least * (amount - 1)
    while spare > 0:
        candidates = [i for i in range(1, amount) if given[i] < largest] or [i for i in range(1, amount) if given[i] < bound]
        whole, budget = sum([loads[i] for i in candidates]), spare
        for i in candidates:
            addition = min(bound - given[i], max(1, budget * loads[i] // whole), spare)
            given[i] = given[i] + addition
            spare = spare - addition
    return np.array(given)


def bell_draw(key, extent, deviation, reach, pieces=(), dtype=jnp.bfloat16):
    result = deviation * jax.random.normal(key, extent, jnp.float32)
    if pieces:
        result = result * block_scale(key, extent, pieces, -0.22, 0.18)
    return jnp.clip(result, -reach, reach).astype(dtype)


def setup_inputs(seed: int = 0) -> dict:
    key_list = jax.random.split(jax.random.key(seed), 10)
    table = bell_draw(key_list[0], (ROWS, D), 1.0, 6.0, ((0, 8),), jnp.float32)
    accum = jnp.clip(jnp.exp(math.log(0.01) - 4.6051702 * jax.random.uniform(key_list[1], (ROWS,), jnp.float32) ** block_scale(key_list[1], (ROWS,), ((0, 8),), -0.2, 0.2)), 0.0001, 0.01)
    owner_keys = jax.random.split(jax.random.fold_in(key_list[2], 1), TOKENS // TOK_DEV)
    owner_turns = jax.random.permutation(jax.random.fold_in(key_list[2], 3), TOKENS // TOK_DEV)
    owner = jax.vmap(lambda own, number: routed_block(jax.random.fold_in(key_list[2], 2), own, number, TOK_DEV, N_SHARD, 1, CAP, 2))(owner_keys, owner_turns).reshape((TOKENS, 1))
    local_row = set_ends(jax.random.randint(key_list[3], (TOKENS,), 0, ROWS_DEV), jax.random.fold_in(key_list[3], 1), 0, ROWS_DEV - 1).astype(jnp.int32)
    lengths = jax.vmap(lambda own: uneven_parts(own, NSEQ, TOK_DEV, MAXLEN, 2))(jax.random.split(key_list[4], (N_REPLICA * N_SHARD))).reshape((N_REPLICA * N_SHARD, NSEQ)).astype(jnp.int32)
    queries = bell_draw(key_list[5], (TOKENS, HEADS * DQK), 1.0, 6.0, ((0, 32),))
    keys = bell_draw(key_list[6], (TOKENS, HEADS * DQK), 1.0, 6.0, ((0, 32),))
    cotangent = bell_draw(key_list[7], (TOKENS, DOUT), 1.0, 6.0, ((0, 32),))
    out_weight = bell_draw(key_list[8], (D, DOUT), DOUT ** -0.5, 0.1875, ((0, 8),))
    return {"table": table, "accum": accum, "owner": owner, "local_row": local_row, "lengths": lengths, "queries": queries, "keys": keys, "cotangent": cotangent, "out_weight": out_weight}


def block_attention(args):
    emb, qry, kys, back, lens = args
    tok = emb.shape[0]
    ends = jnp.cumsum(lens)
    pos = jnp.arange(tok)
    seg = lax.optimization_barrier(jnp.sum((pos[:, None] >= ends[None, :]).astype(jnp.int32), axis=1))
    mask = ((seg[:, None] == seg[None, :]) & (pos[None, :] <= pos[:, None])).astype(jnp.float32)
    q3 = qry.reshape(tok, HEADS, DQK).astype(jnp.float32)
    k3 = kys.reshape(tok, HEADS, DQK).astype(jnp.float32)
    scores = jnp.einsum('ihd,jhd->hij', q3, k3) * DQK ** (-0.5)
    weights = (jax.nn.silu(scores) / MAXLEN * mask[None]).astype(jnp.bfloat16)
    vals = emb.reshape(tok, HEADS, DV).astype(jnp.float32)
    mixed = jnp.einsum('hij,jhd->ihd', weights.astype(jnp.float32), vals).reshape(tok, D).astype(jnp.bfloat16)
    b3 = back.reshape(tok, HEADS, DV).astype(jnp.float32)
    token_grad = jnp.einsum('hij,ihd->jhd', weights.astype(jnp.float32), b3).reshape(tok, D)
    return (mixed, token_grad)

def reference(table, accum, owner, local_row, lengths, queries, keys, cotangent, out_weight):
    devs = N_REPLICA * N_SHARD
    ids = (owner[:, 0] * ROWS_DEV + local_row).astype(jnp.int32)
    rows = jnp.take(table, ids, axis=0).astype(jnp.bfloat16)
    back = jnp.dot(cotangent, out_weight.T, preferred_element_type=jnp.float32).astype(jnp.bfloat16)
    mixed, token_grad = lax.map(block_attention, (rows.reshape(devs, TOK_DEV, D), queries.reshape(devs, TOK_DEV, HEADS * DQK), keys.reshape(devs, TOK_DEV, HEADS * DQK), back.reshape(devs, TOK_DEV, D), lengths))
    mixed = mixed.reshape(TOKENS, D)
    weight_grad = jnp.dot(mixed.T, cotangent, preferred_element_type=jnp.float32).astype(jnp.bfloat16)
    row_grad = jnp.zeros((ROWS, D), jnp.float32).at[ids].add(token_grad.reshape(TOKENS, D))
    new_accum = accum + lax.optimization_barrier(jnp.mean(row_grad * row_grad, axis=1))
    new_table = table - 1.0 * row_grad / (jnp.sqrt(new_accum)[:, None] + 1e-08)
    return (new_table, new_accum, weight_grad)
```

```python
import functools

import jax
import jax.numpy as jnp
from jax import lax
from jax.experimental import pallas as pl
from jax.experimental.pallas import tpu as pltpu
from jax.sharding import PartitionSpec as P

HEADS = 8
MAXLEN = 128
EXTRA = 16
VMEM = pl.BlockSpec(memory_space=pltpu.VMEM)
SMEM = pl.BlockSpec(memory_space=pltpu.SMEM)
F32 = jnp.float32
BF16 = jnp.bfloat16


def adagrad(table_rows, accum_rows, grad_rows):
    new_accum = accum_rows + jnp.mean(grad_rows * grad_rows, axis=1)
    new_table = table_rows - 1.0 * grad_rows / (jnp.sqrt(new_accum)[:, None] + 1e-08)
    return (new_table, new_accum)


def general_body(
    table, accum, owner, local_row, lengths, queries, keys, cotangent, out_weight
):
    shards = lax.axis_size("shard")
    tok = owner.shape[0]
    rows_dev = table.shape[0]
    width = table.shape[1]
    heads = HEADS
    dqk = queries.shape[1] // heads
    dval = width // heads
    slots = 2 * tok // shards
    dest = owner[:, 0]
    onehot = (dest[:, None] == jnp.arange(shards)[None, :]).astype(jnp.bfloat16)
    pos = jnp.arange(tok)
    lower = (pos[None, :] < pos[:, None]).astype(jnp.bfloat16)
    before = jnp.dot(lower, onehot, preferred_element_type=jnp.float32)
    rank = jnp.sum(before * onehot.astype(jnp.float32), axis=1).astype(jnp.int32)
    slot = dest * slots + rank
    send_idx = (
        jnp.full((shards * slots,), -1, jnp.int32).at[slot].set(local_row).reshape(shards, slots)
    )
    recv_idx = lax.all_to_all(send_idx, "shard", split_axis=0, concat_axis=0, tiled=True).reshape(
        -1
    )
    valid = recv_idx >= 0
    picked = jnp.take(table, jnp.clip(recv_idx, 0, rows_dev - 1), axis=0)
    picked = (
        jnp.where(valid[:, None], picked, 0.0).astype(jnp.bfloat16).reshape(shards, slots, width)
    )
    ends = jnp.cumsum(lengths[0])
    seg = jnp.sum((pos[:, None] >= ends[None, :]).astype(jnp.int32), axis=1)
    mask = ((seg[:, None] == seg[None, :]) & (pos[None, :] <= pos[:, None])).astype(jnp.float32)
    q3 = queries.reshape(tok, heads, dqk)
    k3 = keys.reshape(tok, heads, dqk)
    scores = jnp.einsum("ihd,jhd->hij", q3, k3, preferred_element_type=jnp.float32) * dqk ** (-0.5)
    weights = (jax.nn.silu(scores) / MAXLEN * mask[None]).astype(jnp.bfloat16)
    fetched = lax.all_to_all(picked, "shard", split_axis=0, concat_axis=0, tiled=True).reshape(
        shards * slots, width
    )
    embedded = fetched[slot]
    vals = embedded.reshape(tok, heads, dval)
    mixed = (
        jnp.einsum("hij,jhd->ihd", weights, vals, preferred_element_type=jnp.float32)
        .reshape(tok, width)
        .astype(jnp.bfloat16)
    )
    back = lax.dot_general(
        cotangent,
        lax.all_gather(out_weight, "shard", axis=0, tiled=True),
        (((1,), (1,)), ((), ())),
        preferred_element_type=jnp.float32,
    ).astype(jnp.bfloat16)
    grad_share = lax.psum_scatter(
        lax.dot_general(
            mixed, cotangent, (((0,), (0,)), ((), ())), preferred_element_type=jnp.float32
        ),
        "shard",
        scatter_dimension=0,
        tiled=True,
    )
    weight_grad = lax.psum(grad_share, "replica").astype(jnp.bfloat16)
    b3 = back.reshape(tok, heads, dval)
    token_grad = jnp.einsum(
        "hij,ihd->jhd", weights, b3, preferred_element_type=jnp.float32
    ).reshape(tok, width)
    send_grad = (
        jnp.zeros((shards * slots, width), jnp.float32)
        .at[slot]
        .set(token_grad)
        .reshape(shards, slots, width)
    )
    arrived = (
        lax.all_to_all(
            send_grad.astype(jnp.bfloat16), "shard", split_axis=0, concat_axis=0, tiled=True
        )
        .astype(send_grad.dtype)
        .reshape(shards * slots, width)
    )
    select = (recv_idx[:, None] == jnp.arange(rows_dev)[None, :]).astype(jnp.float32)
    grad_rows = lax.dot_general(
        select,
        arrived,
        (((0,), (0,)), ((), ())),
        precision=lax.Precision.HIGHEST,
        preferred_element_type=jnp.float32,
    )
    share = lax.psum_scatter(
        grad_rows.astype(jnp.bfloat16), "replica", scatter_dimension=0, tiled=True
    ).astype(jnp.float32)
    quarter = share.shape[0]
    first = lax.axis_index("replica") * quarter
    part_table = lax.dynamic_slice_in_dim(table, first, quarter, 0)
    part_accum = lax.dynamic_slice_in_dim(accum, first, quarter, 0)
    upd_table, upd_accum = adagrad(part_table, part_accum, share)
    new_table, new_accum = (
        lax.all_gather(upd_table, "replica", axis=0, tiled=True),
        lax.all_gather(upd_accum, "replica", axis=0, tiled=True),
    )
    return (new_table, new_accum, weight_grad)


def iota(shape, axis):
    return lax.broadcasted_iota(jnp.int32, shape, axis)


def nt(a, b):
    return lax.dot_general(a, b, (((1,), (1,)), ((), ())), preferred_element_type=F32)


def nn(a, b):
    return lax.dot_general(a, b, (((1,), (0,)), ((), ())), preferred_element_type=F32)


def call(kernel, name, out, n_in, smem=1, scratch=(), flops=0, nbytes=0):
    return pl.pallas_call(
        kernel,
        out_shape=out,
        in_specs=[SMEM] * smem + [VMEM] * n_in,
        out_specs=[VMEM] * len(out) if isinstance(out, (list, tuple)) else VMEM,
        scratch_shapes=list(scratch),
        name=name,
        cost_estimate=pl.CostEstimate(flops=flops, bytes_accessed=nbytes, transcendentals=0),
        compiler_params=pltpu.CompilerParams(vmem_limit_bytes=32 * 1024 * 1024),
    )


def sds(shape, dtype=BF16):
    return jax.ShapeDtypeStruct(shape, dtype)


def pack_kernel(me, lens, q, k, owner, local, *out):
    tok = q.shape[0]
    pw = q.shape[1] // len(out)
    lane = iota((EXTRA, tok), 1)
    row = iota((EXTRA, tok), 0)
    seg = jnp.zeros((EXTRA, tok), F32)
    end = jnp.int32(0)
    for n in range(lens.shape[1]):
        end = end + lens[0, n]
        seg = seg + jnp.where(lane >= end, 1.0, 0.0)
    own = jnp.broadcast_to(owner[...].astype(F32), (EXTRA, tok))
    loc = jnp.broadcast_to(local[...].astype(F32), (EXTRA, tok))
    ids = jnp.where(row == 0, own, jnp.where(row == 1, loc, jnp.where(row == 2, seg, 0.0)))
    ids = ids.astype(BF16)
    for n, o in enumerate(out):
        at = pl.ds(pl.multiple_of((me[0] ^ n) * pw, pw), pw)
        o[0:tok, 0:pw] = q[:, at]
        o[0:tok, pw : 2 * pw] = k[:, at]
        o[tok : tok + EXTRA, :] = ids


def rows_kernel(me, table, weight, out_t, out_z):
    rows, width = table.shape
    cols = out_t.shape[0]
    at = pl.ds(pl.multiple_of(me[0] * cols, cols), cols)
    t = table[:, at].T.astype(BF16)
    out_t[...] = t
    out_z[0:cols, :] = t
    part = weight.shape[0] * cols // width
    w = weight[pl.ds(pl.multiple_of(me[0] * part, part), part), :]
    for n in range(width // rows):
        out_z[cols + n * part : cols + (n + 1) * part, :] = w[:, n * rows : (n + 1) * rows]


def weights_kernel(*refs):
    *packs, out = refs
    tok = packs[0].shape[0] - EXTRA
    pw = packs[0].shape[1] // 2
    heads = out.shape[1]
    dqk = pw // heads
    down, across = iota((tok, tok), 0), iota((tok, tok), 1)
    lane = iota((tok, pw), 1)
    for r, p in enumerate(packs):
        q = p[0:tok, 0:pw]
        k = p[0:tok, pw : 2 * pw]
        seg = p[tok : tok + EXTRA, :].astype(F32)[2:3, :]
        seg_down = jnp.sum(jnp.where(down == across, seg, 0.0), axis=1, keepdims=True)
        mask = (seg == seg_down) & (down <= across)
        for j in range(heads):
            kj = jnp.where(lane // dqk == j, k, jnp.zeros_like(k))
            s = nt(kj, q) * dqk ** (-0.5)
            w = s / (1.0 + jnp.exp(-s)) * (1.0 / MAXLEN)
            out[r, j] = jnp.where(mask, w, 0.0).astype(BF16)


def choose_kernel(me, *refs):
    n = len(refs) // 2
    parts, out = refs[:n], refs[n : 2 * n]
    held = refs[2 * n]
    first = held.shape[1]
    first = parts[0].shape[0] - first
    for m in range(n):
        held[m] = parts[m][first:, :]
    for m in range(n):
        out[m][...] = held[me[1] ^ me[0] ^ m]


def pick_kernel(me, *refs):
    n = (len(refs) - 1) // 2
    held = refs[2 * n]
    for m in range(n):
        held[m] = refs[m][...]
    for m in range(n):
        refs[n + m][...] = held[me[1] ^ me[0] ^ m]


def one_hot(ids, rows):
    tok = ids.shape[1]
    own = ids[0:1, :]
    loc = ids[1:2, :]
    at = iota((rows, tok), 0).astype(F32)
    return jnp.broadcast_to(own, (rows, tok)), at == loc


def mix_kernel(n, me, *refs):
    mine, other = refs[:n], refs[n : 2 * n]
    packs = refs[2 * n : 3 * n]
    w, out = refs[3 * n], refs[3 * n + 1]
    cols = other[0].shape[0]
    rows = other[0].shape[1]
    tok = packs[0].shape[0] - EXTRA
    heads = w.shape[1]
    dv = cols // heads
    for r in range(n):
        ids = packs[r][tok : tok + EXTRA, :].astype(F32)
        own, hit = one_hot(ids, rows)
        vals = jnp.zeros((cols, tok), F32)
        for m in range(n):
            for cc in range(2):
                shard = (2 * (me[1] ^ m) + (me[2] ^ cc)).astype(F32)
                pickm = jnp.where(hit & (own == shard), 1.0, 0.0).astype(BF16)
                block = mine[m][0:cols, :] if cc == 0 else other[m][...]
                vals = vals + nn(block, pickm)
        vals = vals.astype(BF16)
        for j in range(heads):
            out[j * dv : (j + 1) * dv, r * tok : (r + 1) * tok] = nn(
                vals[j * dv : (j + 1) * dv, :], w[r, j]
            ).astype(BF16)


def back_kernel(n, me, *refs):
    cots, packs = refs[:n], refs[n : 2 * n]
    ow_mine, ow_other, w = refs[2 * n : 2 * n + 3]
    keep, send = refs[2 * n + 3 : 2 * n + 5]
    ow, grad = refs[2 * n + 5 :]
    tok = cots[0].shape[0]
    heads = w.shape[1]
    head_rows = ow_mine.shape[0]
    part = head_rows // n
    rows = send.shape[1]
    for cc, src in enumerate((ow_mine, ow_other)):
        for m in range(n):
            at = (me[2] ^ cc) * head_rows + (me[0] ^ m) * part
            ow[pl.ds(pl.multiple_of(at, part), part), :] = src[m * part : (m + 1) * part, :]
    for r in range(n):
        back = nt(cots[r][...], ow[...]).astype(BF16)
        for j in range(heads):
            at = slice(j * head_rows, (j + 1) * head_rows)
            grad[r * tok : (r + 1) * tok, at] = nn(w[r, j], back[:, at]).astype(BF16)
    for m in range(n):
        for cc in range(2):
            shard = (2 * (me[1] ^ m) + (me[2] ^ cc)).astype(F32)
            total = jnp.zeros((rows, heads * head_rows), F32)
            for r in range(n):
                ids = packs[r][tok : tok + EXTRA, :].astype(F32)
                own, hit = one_hot(ids, rows)
                pickm = jnp.where(hit & (own == shard), 1.0, 0.0).astype(BF16)
                total = total + nn(pickm, grad[r * tok : (r + 1) * tok, :])
            if cc == 0:
                keep[m] = total
            else:
                send[m] = total.astype(BF16)


def wgrad_kernel(n, me, mixed, *refs):
    cots, (keep, send) = refs[:n], refs[n:]
    tok = cots[0].shape[0]
    rows = keep.shape[0]
    for cc, out in ((1, send), (0, keep)):
        at = pl.ds(pl.multiple_of((me[2] ^ cc) * rows, rows), rows)
        total = jnp.zeros(keep.shape, F32)
        for r in range(n):
            total = total + nn(mixed[at, r * tok : (r + 1) * tok], cots[r][...])
        out[...] = total.astype(out.dtype)


def add_kernel(keep, got, *out):
    for m, o in enumerate(out):
        o[...] = (keep[m] + got[m].astype(F32)).astype(o.dtype)


def add_parts_kernel(me, keep, got, *out):
    n = len(out)
    part = keep.shape[0] // n
    for m, o in enumerate(out):
        at = pl.ds(pl.multiple_of((me[0] ^ m) * part, part), part)
        o[...] = (keep[at, :] + got[at, :].astype(F32)).astype(o.dtype)


def sum_kernel(*refs):
    *parts, out = refs
    total = parts[0][...].astype(F32)
    for p in parts[1:]:
        total = total + p[...].astype(F32)
    out[...] = total.astype(out.dtype)


def place_kernel(me, *refs):
    *parts, out = refs
    rows = parts[0].shape[0]
    for m, p in enumerate(parts):
        out[pl.ds(pl.multiple_of((me[0] ^ m) * rows, rows), rows), :] = p[...]


def update_kernel(n, me, *refs):
    parts = refs[:n]
    table, accum, new_table, new_accum, grad = refs[n:]
    rows, width = table.shape
    cols = width // n
    for m in range(n):
        at = pl.ds(pl.multiple_of((me[0] ^ m) * cols, cols), cols)
        grad[:, at] = parts[m][...].astype(F32)
    mean = jnp.sum(grad[...] * grad[...], axis=1, keepdims=True) * (1.0 / width)
    same = iota((rows, rows), 0) == iota((rows, rows), 1)
    old = jnp.sum(jnp.where(same, accum[...], 0.0), axis=1, keepdims=True)
    fresh = old + mean
    new_accum[...] = jnp.sum(jnp.where(same, fresh, 0.0), axis=0, keepdims=True)
    new_table[...] = table[...] - grad[...] / (jnp.sqrt(fresh) + 1e-08)


def body(table, accum, owner, local_row, lengths, queries, keys, cotangent, out_weight):
    n = lax.axis_size("replica")
    shards = lax.axis_size("shard")
    tok = owner.shape[0]
    rows, width = table.shape
    cols = width // n
    heads = HEADS // n
    part = out_weight.shape[0] // n
    shard = lax.axis_index("shard")
    me = jnp.stack([lax.axis_index("replica"), shard // 2, shard % 2]).astype(jnp.int32)

    def column(x, m):
        return lax.ppermute(x, "replica", [(i, i ^ m) for i in range(n)]) if m else x

    def along(x, m):
        return lax.ppermute(x, "shard", [(i, i ^ (2 * m)) for i in range(shards)]) if m else x

    def core(x):
        return lax.ppermute(x, "shard", [(i, i ^ 1) for i in range(shards)])

    packs = call(
        pack_kernel,
        "pack",
        [sds((tok + EXTRA, 2 * queries.shape[1] // n))] * n,
        4,
        smem=2,
    )(me, lengths, queries, keys, owner.reshape(1, tok), local_row.reshape(1, tok))
    packs = [column(p, m) for m, p in enumerate(packs)]
    cots = [column(cotangent, m) for m in range(n)]

    zrows = cols + part * width // rows
    turned, zpay = call(
        rows_kernel, "rows", [sds((cols, rows)), sds((zrows, rows))], 2
    )(me, table, out_weight)
    mine = [along(zpay, m) for m in range(n)]
    other = [core(turned if m == 0 else mine[m][0:cols]) for m in range(n)]

    w = call(
        weights_kernel, "weights", sds((n, heads, tok, tok)), n, smem=0, flops=n * heads * tok * tok * 512
    )(*packs)

    owp = call(
        choose_kernel,
        "choose",
        [sds((zrows - cols, rows))] * n,
        n,
        scratch=[pltpu.VMEM((n, zrows - cols, rows), BF16)],
    )(me, *mine)
    owp = [column(p, m) for m, p in enumerate(owp)]
    owp = [
        jnp.concatenate([p[i * part : (i + 1) * part] for i in range(width // rows)], axis=1)
        for p in owp
    ]
    ow_mine = jnp.concatenate(owp, axis=0)
    ow_other = core(ow_mine)

    mixed = call(
        functools.partial(mix_kernel, n), "mix", sds((cols, n * tok)), 3 * n + 1, flops=2 * n * tok * cols * rows * shards
    )(me, *mine, *other, *packs, w)

    keep, send = call(
        functools.partial(back_kernel, n),
        "back",
        [sds((n, rows, cols), F32), sds((n, rows, cols))],
        2 * n + 3,
        scratch=[pltpu.VMEM((cols, width), BF16), pltpu.VMEM((n * tok, cols), BF16)],
        flops=4 * n * tok * cols * width,
    )(me, *cots, *packs, ow_mine, ow_other, w)
    got = core(send)
    sums = call(
        add_kernel, "add", [sds((rows, cols), F32)] + [sds((rows, cols))] * (n - 1), 2, smem=0
    )(keep, got)
    sums = [along(s, m) for m, s in enumerate(sums)]
    grad = call(sum_kernel, "sum_rows", sds((rows, cols)), n, smem=0)(*sums)
    grads = [column(grad, m) for m in range(n)]
    new_table, new_accum = call(
        functools.partial(update_kernel, n),
        "update",
        [sds((rows, width), F32), sds((1, rows), F32)],
        n + 2,
        scratch=[pltpu.VMEM((rows, width), F32)],
    )(me, *grads, table, accum.reshape(1, rows))

    wkeep, wsend = call(
        functools.partial(wgrad_kernel, n),
        "wgrad",
        [sds((n * part, width), F32), sds((n * part, width))],
        n + 1,
        flops=2 * n * tok * cols * width,
    )(me, mixed, *cots)
    wparts = call(add_parts_kernel, "add_parts", [sds((part, width))] * n, 2)(
        me, wkeep, core(wsend)
    )
    wparts = [column(p, m) for m, p in enumerate(wparts)]
    wparts = call(
        pick_kernel,
        "pick",
        [sds((part, width))] * n,
        n,
        scratch=[pltpu.VMEM((n, part, width), BF16)],
    )(me, *wparts)
    wparts = [along(p, m) for m, p in enumerate(wparts)]
    wsum = call(sum_kernel, "sum_parts", sds((part, width)), n, smem=0)(*wparts)
    wsums = [column(wsum, m) for m in range(n)]
    weight_grad = call(place_kernel, "place", sds((n * part, width)), n)(me, *wsums)
    return (new_table, new_accum.reshape(rows), weight_grad)


def fits(mesh):
    n, shards = mesh.shape["replica"], mesh.shape["shard"]
    return n & (n - 1) == 0 and shards == HEADS and 2 * n == HEADS


def solution(mesh):
    placed = (
        P("shard", None),
        P("shard"),
        P(("replica", "shard"), None),
        P(("replica", "shard")),
        P(("replica", "shard"), None),
        P(("replica", "shard"), None),
        P(("replica", "shard"), None),
        P(("replica", "shard"), None),
        P("shard", None),
    )
    return jax.shard_map(
        body if fits(mesh) else general_body,
        mesh=mesh,
        in_specs=placed,
        out_specs=(P("shard", None), P("shard"), P("shard", None)),
        check_vma=False,
    )
```

```python
import functools

import jax
import jax.numpy as jnp
from jax import lax
from jax.experimental import pallas as pl
from jax.experimental.pallas import tpu as pltpu
from jax.sharding import PartitionSpec as P

HEADS = 8
MAXLEN = 128
PASS_COST = 12 * 10**9
GATE_COST = 8 * 10**9
EXTRA = 16
VMEM = pl.BlockSpec(memory_space=pltpu.VMEM)
ANY = pl.BlockSpec(memory_space=pl.ANY)
HBM = pl.BlockSpec(memory_space=pltpu.HBM)
SMEM = pl.BlockSpec(memory_space=pltpu.SMEM)
F32 = jnp.float32
BF16 = jnp.bfloat16


def adagrad(table_rows, accum_rows, grad_rows):
    new_accum = accum_rows + jnp.mean(grad_rows * grad_rows, axis=1)
    new_table = table_rows - 1.0 * grad_rows / (jnp.sqrt(new_accum)[:, None] + 1e-08)
    return (new_table, new_accum)


def general_body(
    table, accum, owner, local_row, lengths, queries, keys, cotangent, out_weight
):
    shards = lax.axis_size("shard")
    tok = owner.shape[0]
    rows_dev = table.shape[0]
    width = table.shape[1]
    heads = HEADS
    dqk = queries.shape[1] // heads
    dval = width // heads
    slots = 2 * tok // shards
    dest = owner[:, 0]
    onehot = (dest[:, None] == jnp.arange(shards)[None, :]).astype(jnp.bfloat16)
    pos = jnp.arange(tok)
    lower = (pos[None, :] < pos[:, None]).astype(jnp.bfloat16)
    before = jnp.dot(lower, onehot, preferred_element_type=jnp.float32)
    rank = jnp.sum(before * onehot.astype(jnp.float32), axis=1).astype(jnp.int32)
    slot = dest * slots + rank
    send_idx = (
        jnp.full((shards * slots,), -1, jnp.int32).at[slot].set(local_row).reshape(shards, slots)
    )
    recv_idx = lax.all_to_all(send_idx, "shard", split_axis=0, concat_axis=0, tiled=True).reshape(
        -1
    )
    valid = recv_idx >= 0
    picked = jnp.take(table, jnp.clip(recv_idx, 0, rows_dev - 1), axis=0)
    picked = (
        jnp.where(valid[:, None], picked, 0.0).astype(jnp.bfloat16).reshape(shards, slots, width)
    )
    ends = jnp.cumsum(lengths[0])
    seg = jnp.sum((pos[:, None] >= ends[None, :]).astype(jnp.int32), axis=1)
    mask = ((seg[:, None] == seg[None, :]) & (pos[None, :] <= pos[:, None])).astype(jnp.float32)
    q3 = queries.reshape(tok, heads, dqk)
    k3 = keys.reshape(tok, heads, dqk)
    scores = jnp.einsum("ihd,jhd->hij", q3, k3, preferred_element_type=jnp.float32) * dqk ** (-0.5)
    weights = (jax.nn.silu(scores) / MAXLEN * mask[None]).astype(jnp.bfloat16)
    fetched = lax.all_to_all(picked, "shard", split_axis=0, concat_axis=0, tiled=True).reshape(
        shards * slots, width
    )
    embedded = fetched[slot]
    vals = embedded.reshape(tok, heads, dval)
    mixed = (
        jnp.einsum("hij,jhd->ihd", weights, vals, preferred_element_type=jnp.float32)
        .reshape(tok, width)
        .astype(jnp.bfloat16)
    )
    back = lax.dot_general(
        cotangent,
        lax.all_gather(out_weight, "shard", axis=0, tiled=True),
        (((1,), (1,)), ((), ())),
        preferred_element_type=jnp.float32,
    ).astype(jnp.bfloat16)
    grad_share = lax.psum_scatter(
        lax.dot_general(
            mixed, cotangent, (((0,), (0,)), ((), ())), preferred_element_type=jnp.float32
        ),
        "shard",
        scatter_dimension=0,
        tiled=True,
    )
    weight_grad = lax.psum(grad_share, "replica").astype(jnp.bfloat16)
    b3 = back.reshape(tok, heads, dval)
    token_grad = jnp.einsum(
        "hij,ihd->jhd", weights, b3, preferred_element_type=jnp.float32
    ).reshape(tok, width)
    send_grad = (
        jnp.zeros((shards * slots, width), jnp.float32)
        .at[slot]
        .set(token_grad)
        .reshape(shards, slots, width)
    )
    arrived = (
        lax.all_to_all(
            send_grad.astype(jnp.bfloat16), "shard", split_axis=0, concat_axis=0, tiled=True
        )
        .astype(send_grad.dtype)
        .reshape(shards * slots, width)
    )
    select = (recv_idx[:, None] == jnp.arange(rows_dev)[None, :]).astype(jnp.float32)
    grad_rows = lax.dot_general(
        select,
        arrived,
        (((0,), (0,)), ((), ())),
        precision=lax.Precision.HIGHEST,
        preferred_element_type=jnp.float32,
    )
    share = lax.psum_scatter(
        grad_rows.astype(jnp.bfloat16), "replica", scatter_dimension=0, tiled=True
    ).astype(jnp.float32)
    quarter = share.shape[0]
    first = lax.axis_index("replica") * quarter
    part_table = lax.dynamic_slice_in_dim(table, first, quarter, 0)
    part_accum = lax.dynamic_slice_in_dim(accum, first, quarter, 0)
    upd_table, upd_accum = adagrad(part_table, part_accum, share)
    new_table, new_accum = (
        lax.all_gather(upd_table, "replica", axis=0, tiled=True),
        lax.all_gather(upd_accum, "replica", axis=0, tiled=True),
    )
    return (new_table, new_accum, weight_grad)


def iota(shape, axis):
    return lax.broadcasted_iota(jnp.int32, shape, axis)


def nt(a, b):
    return lax.dot_general(a, b, (((1,), (1,)), ((), ())), preferred_element_type=F32)


def nn(a, b):
    return lax.dot_general(a, b, (((1,), (0,)), ((), ())), preferred_element_type=F32)


def call(kernel, name, out, ins, smem=0, after=(), scratch=(), hbm=(), limit=32 << 20, cost=0, placed=False):
    n_in, n_after = len(ins), len(after)
    many = isinstance(out, (list, tuple))

    def run(*refs):
        refs = (*refs[:n_in], *refs[n_in + n_after :])
        if placed:
            shard = lax.axis_index("shard")
            kernel((lax.axis_index("replica"), shard // 2, shard % 2), *refs)
        else:
            kernel(*refs)

    return pl.pallas_call(
        run,
        out_shape=out,
        in_specs=[SMEM if i < smem else HBM if i in hbm else VMEM for i in range(n_in)]
        + [ANY] * n_after,
        out_specs=[VMEM] * len(out) if many else VMEM,
        scratch_shapes=list(scratch),
        name=name,
        cost_estimate=pl.CostEstimate(flops=cost, bytes_accessed=0, transcendentals=0),
        compiler_params=pltpu.CompilerParams(vmem_limit_bytes=limit),
    )(*ins, *after)


def sds(shape, dtype=BF16):
    return jax.ShapeDtypeStruct(shape, dtype)


def aligned(index, size):
    return pl.ds(pl.multiple_of(index * size, size), size)


def start_all(pairs, sem):
    copies = [pltpu.make_async_copy(a, b, sem.at[i]) for i, (a, b) in enumerate(pairs)]
    for c in copies:
        c.start()
    return copies


def pack_kernel(me, lens, owner, local, q, k, weight, table, out, out_z, rows_in, part_in, sem):
    n, _, pw = out.shape
    pw = pw // 2
    tok = q.shape[0]
    rows, cols = rows_in.shape
    part = part_in.shape[0]
    copies = start_all(
        [
            (table.at[:, aligned(me[0], cols)], rows_in),
            (weight.at[aligned(me[0], part), :], part_in),
        ]
        + [
            (x.at[:, i * pw : (i + 1) * pw], out.at[i, 0:tok, j * pw : (j + 1) * pw])
            for i in range(n)
            for j, x in enumerate((q, k))
        ],
        sem,
    )
    lane = iota((EXTRA, tok), 1)
    row = iota((EXTRA, tok), 0)
    seg = jnp.zeros((EXTRA, tok), F32)
    end = jnp.int32(0)
    for i in range(lens.shape[1]):
        end = end + lens[0, i]
        seg = seg + jnp.where(lane >= end, 1.0, 0.0)
    ids = jnp.where(
        row == 0,
        jnp.broadcast_to(owner[...].astype(F32), (EXTRA, tok)),
        jnp.where(
            row == 1,
            jnp.broadcast_to(local[...].astype(F32), (EXTRA, tok)),
            jnp.where(row == 2, seg, 0.0),
        ),
    ).astype(BF16)
    for i in range(n):
        out[i, tok : tok + EXTRA, :] = ids
    copies[0].wait()
    out_z[0:cols, :] = rows_in[...].T.astype(BF16)
    copies[1].wait()
    for i in range((out_z.shape[0] - cols) // part):
        out_z[cols + i * part : cols + (i + 1) * part, :] = part_in[:, i * rows : (i + 1) * rows]
    for c in copies[2:]:
        c.wait()


def pass_kernel(x, y, far_y, far_x, sem):
    half = far_x.shape[0]
    copies = start_all([(x.at[half:, :], far_y), (y.at[0:half, :], far_x)], sem)
    for c in copies:
        c.wait()


def sort_kernel(me, *refs):
    *blocks, out_t, out_w = refs
    _, cols, rows = out_t.shape
    part = out_w.shape[1]
    for m, p in enumerate(blocks):
        z = me[1] ^ m
        out_t[z] = p[0:cols, :]
        for i in range((p.shape[0] - cols) // part):
            out_w[z, :, i * rows : (i + 1) * rows] = p[cols + i * part : cols + (i + 1) * part, :]


def gate_kernel(out):
    out[...] = jnp.zeros_like(out)


def choose_kernel(me, *refs):
    n = (len(refs) - 1) // 2
    parts, out, held = refs[:n], refs[n : 2 * n], refs[2 * n]
    for m, p in enumerate(parts):
        held[m] = p[...]
    for m, o in enumerate(out):
        o[...] = held[me[1] ^ me[0] ^ m]


def weights_kernel(me, packs, out):
    n, tok, pw = packs.shape
    tok, pw = tok - EXTRA, pw // 2
    heads = out.shape[1]
    dqk = pw // heads
    down, across = iota((tok, tok), 0), iota((tok, tok), 1)
    lane = iota((tok, pw), 1)
    for r in range(n):
        p = packs.at[me[0] ^ r]
        q = p[0:tok, 0:pw]
        k = p[0:tok, pw : 2 * pw]
        seg = ids_of(packs, me[0] ^ r)[2:3, :]
        seg_down = jnp.sum(jnp.where(down == across, seg, 0.0), axis=1, keepdims=True)
        mask = (seg == seg_down) & (down <= across)
        for j in range(heads):
            kj = jnp.where(lane // dqk == j, k, jnp.zeros_like(k))
            s = nt(kj, q) * dqk ** (-0.5)
            w = s / (1.0 + jnp.exp(-s)) * (1.0 / MAXLEN)
            out[r, j] = jnp.where(mask, w, 0.0).astype(BF16)


def ids_of(packs, r):
    rows = packs.shape[1]
    return packs[r, rows - EXTRA : rows, :].astype(F32)


def one_hot(ids, rows):
    tok = ids.shape[1]
    own = ids[0:1, :]
    loc = ids[1:2, :]
    at = iota((rows, tok), 0).astype(F32)
    return jnp.broadcast_to(own, (rows, tok)), at == loc


def mix_kernel(me, packs, w, mine, other, out):
    n, cols, rows = mine.shape
    heads, tok = w.shape[1:3]
    dv = cols // heads
    for r in range(n):
        own, hit = one_hot(ids_of(packs, me[0] ^ r), rows)
        vals = jnp.zeros((cols, tok), F32)
        for z in range(n):
            for cc, blocks in enumerate((mine, other)):
                shard = (2 * z + (me[2] ^ cc)).astype(F32)
                pick = jnp.where(hit & (own == shard), 1.0, 0.0).astype(BF16)
                vals = vals + nn(blocks[z], pick)
        vals = vals.astype(BF16)
        for j in range(heads):
            out[j * dv : (j + 1) * dv, r * tok : (r + 1) * tok] = nn(
                vals[j * dv : (j + 1) * dv, :], w[r, j]
            ).astype(BF16)


def back_kernel(me, packs, ow_mine, ow_other, w, *refs):
    *cots, keep, send, ow, grad = refs
    n = packs.shape[0]
    heads, tok = w.shape[1:3]
    head_rows = ow_mine.shape[0]
    rows = send.shape[1]
    ow[aligned(me[2], head_rows), :] = ow_mine[...]
    ow[aligned(1 - me[2], head_rows), :] = ow_other[...]
    first = 0
    for cot in cots:
        end = first + cot.shape[0]
        grad[first:end, :] = nt(cot[...], ow[...]).astype(BF16)
        first = end
    for r in range(n):
        at_r = slice(r * tok, (r + 1) * tok)
        for j in range(heads):
            at_j = slice(j * head_rows, (j + 1) * head_rows)
            grad[at_r, at_j] = nn(w[r, j], grad[at_r, at_j]).astype(BF16)
    for cc in (1, 0):
        for z in range(n):
            shard = (2 * z + (me[2] ^ cc)).astype(F32)
            total = jnp.zeros((rows, heads * head_rows), F32)
            for r in range(n):
                own, hit = one_hot(ids_of(packs, me[0] ^ r), rows)
                pick = jnp.where(hit & (own == shard), 1.0, 0.0).astype(BF16)
                total = total + nn(pick, grad[r * tok : (r + 1) * tok, :])
            if cc == 0:
                keep[z] = total
            else:
                send[z] = total.astype(BF16)


def wgrad_kernel(me, mixed, *refs):
    *cots, keep, send = refs
    rows = keep.shape[0]
    for cc, out in ((1, send), (0, keep)):
        at = aligned(me[2] ^ cc, rows)
        total = jnp.zeros(keep.shape, F32)
        first = 0
        for cot in cots:
            end = first + cot.shape[0]
            total = total + nn(mixed[at, first:end], cot[...])
            first = end
        out[...] = total.astype(out.dtype)


def add_kernel(keep, got, out):
    out[...] = (keep[...] + got[...].astype(F32)).astype(out.dtype)


def add_parts_kernel(me, keep, got, *out):
    rows = out[0].shape[0]
    for m, o in enumerate(out):
        at = aligned(me[0] ^ m, rows)
        o[...] = (keep[at, :] + got[at, :].astype(F32)).astype(o.dtype)


def sum_first_kernel(parts, out):
    total = parts[0].astype(F32)
    for m in range(1, parts.shape[0]):
        total = total + parts[m].astype(F32)
    out[...] = total.astype(out.dtype)


def sum_kernel(*refs):
    *parts, out = refs
    total = parts[0][...].astype(F32)
    for p in parts[1:]:
        total = total + p[...].astype(F32)
    out[...] = total.astype(out.dtype)


def place_kernel(me, *refs):
    *parts, out = refs
    rows = parts[0].shape[0]
    for m, p in enumerate(parts):
        out[aligned(me[0] ^ m, rows), :] = p[...]


def update_kernel(me, table, accum, *refs):
    *parts, new_table, new_accum, grad = refs
    rows, width = table.shape
    cols = width // len(parts)
    for m, p in enumerate(parts):
        grad[:, aligned(me[0] ^ m, cols)] = p[...].astype(F32)
    mean = jnp.sum(grad[...] * grad[...], axis=1, keepdims=True) * (1.0 / width)
    same = iota((rows, rows), 0) == iota((rows, rows), 1)
    old = jnp.sum(jnp.where(same, accum[...], 0.0), axis=1, keepdims=True)
    fresh = old + mean
    new_accum[...] = jnp.sum(jnp.where(same, fresh, 0.0), axis=0, keepdims=True)
    new_table[...] = table[...] - grad[...] / (jnp.sqrt(fresh) + 1e-08)


def body(table, accum, owner, local_row, lengths, queries, keys, cotangent, out_weight):
    n = lax.axis_size("replica")
    shards = lax.axis_size("shard")
    tok = owner.shape[0]
    rows, width = table.shape
    cols = width // n
    heads = HEADS // n
    part = out_weight.shape[0] // n

    def column(x, m):
        return lax.ppermute(x, "replica", [(i, i ^ m) for i in range(n)]) if m else x

    def along(x, m):
        return lax.ppermute(x, "shard", [(i, i ^ (2 * m)) for i in range(shards)]) if m else x

    def core(x):
        return lax.ppermute(x, "shard", [(i, i ^ 1) for i in range(shards)])

    def swap_along(x):
        groups = [list(range(c, shards, 2)) for c in range(2)]
        return lax.all_to_all(x, "shard", 0, 0, tiled=True, axis_index_groups=groups)

    def swap_columns(x):
        return lax.all_to_all(x, "replica", 0, 0, tiled=True)

    half = tok // 2
    x, y = column(cotangent, 1), column(cotangent, 2)
    zrows = cols + part * width // rows
    packs, zpay = call(
        pack_kernel,
        "pack",
        [sds((n, tok + EXTRA, 2 * queries.shape[1] // n)), sds((zrows, rows))],
        (
            lengths,
            owner.reshape(1, tok),
            local_row.reshape(1, tok),
            queries,
            keys,
            out_weight,
            table,
        ),
        smem=1,
        hbm=(3, 4, 5, 6),
        scratch=[
            pltpu.VMEM((rows, cols), F32),
            pltpu.VMEM((part, width), BF16),
            pltpu.SemaphoreType.DMA((2 * n + 2,)),
        ],
        limit=None,
        placed=True,
    )
    packs = swap_columns(packs)
    blocks = [along(zpay, m) for m in range(n)]
    far_y, far_x = call(
        pass_kernel,
        "pass",
        [sds((half, width))] * 2,
        (x, y),
        scratch=[pltpu.SemaphoreType.DMA((2,))],
        cost=PASS_COST,
    )
    w = call(
        weights_kernel,
        "weights",
        sds((n, heads, tok, tok)),
        (packs,),
        after=(far_x,),
        placed=True,
    )
    mine, owp = call(
        sort_kernel,
        "sort",
        [sds((n, cols, rows)), sds((n, part, width))],
        blocks,
        after=(w,),
        placed=True,
    )
    other = core(mine)
    ow_mine = swap_columns(owp).reshape(n * part, width)
    ow_other = core(ow_mine)
    far_y, far_x = column(far_y, 2), column(far_x, 1)
    cots = [cotangent, x, y, far_x, far_y]
    here = call(gate_kernel, "gate", sds((8, 128), F32), (), after=(far_x, far_y), cost=GATE_COST)

    keep, send = call(
        back_kernel,
        "back",
        [sds((n, rows, cols), F32), sds((n, rows, cols))],
        (packs, ow_mine, ow_other, w, *cots),
        after=(here,),
        scratch=[pltpu.VMEM((cols, width), BF16), pltpu.VMEM((n * tok, cols), BF16)],
        placed=True,
    )
    sums = call(add_kernel, "add", sds((n, rows, cols)), (keep, core(send)))
    mixed = call(
        mix_kernel,
        "mix",
        sds((cols, n * tok)),
        (packs, w, mine, other),
        after=(sums,),
        placed=True,
    )
    sums = swap_along(sums)
    wkeep, wsend = call(
        wgrad_kernel,
        "wgrad",
        [sds((n * part, width), F32), sds((n * part, width))],
        (mixed, *cots),
        placed=True,
    )
    wgot = core(wsend)

    wparts = call(
        add_parts_kernel, "add_parts", [sds((part, width))] * n, (wkeep, wgot), placed=True
    )
    wparts = [column(p, m) for m, p in enumerate(wparts)]
    wparts = call(
        choose_kernel,
        "pick",
        [sds((part, width))] * n,
        wparts,
        placed=True,
        scratch=[pltpu.VMEM((n, part, width), BF16)],
    )
    wready = wparts[0]
    wparts = [along(p, m) for m, p in enumerate(wparts)]

    grad = call(sum_first_kernel, "sum_rows", sds((rows, cols)), (sums,), after=(wready,))
    grads = [column(grad, m) for m in range(n)]
    wsum = call(sum_kernel, "sum_parts", sds((part, width)), wparts, after=(grads[1],))
    wsums = [column(wsum, m) for m in range(n)]
    new_table, new_accum = call(
        update_kernel,
        "update",
        [sds((rows, width), F32), sds((1, rows), F32)],
        (table, accum.reshape(1, rows), *grads),
        placed=True,
        scratch=[pltpu.VMEM((rows, width), F32)],
    )
    weight_grad = call(place_kernel, "place", sds((n * part, width)), wsums, placed=True)
    return (new_table, new_accum.reshape(rows), weight_grad)


def fits(mesh):
    n, shards = mesh.shape["replica"], mesh.shape["shard"]
    return n & (n - 1) == 0 and shards == HEADS and 2 * n == HEADS


def solution(mesh):
    placed = (
        P("shard", None),
        P("shard"),
        P(("replica", "shard"), None),
        P(("replica", "shard")),
        P(("replica", "shard"), None),
        P(("replica", "shard"), None),
        P(("replica", "shard"), None),
        P(("replica", "shard"), None),
        P("shard", None),
    )
    return jax.shard_map(
        body if fits(mesh) else general_body,
        mesh=mesh,
        in_specs=placed,
        out_specs=(P("shard", None), P("shard"), P("shard", None)),
        check_vma=False,
    )
```

```python
import functools

import jax
import jax.numpy as jnp
from jax import lax
from jax.experimental import pallas as pl
from jax.experimental.pallas import tpu as pltpu
from jax.sharding import PartitionSpec as P

HEADS = 8
MAXLEN = 128
PASS_COST = 12 * 10**9
GATE_COST = 8 * 10**9
EXTRA = 16
VMEM = pl.BlockSpec(memory_space=pltpu.VMEM)
ANY = pl.BlockSpec(memory_space=pl.ANY)
HBM = pl.BlockSpec(memory_space=pltpu.HBM)
SMEM = pl.BlockSpec(memory_space=pltpu.SMEM)
F32 = jnp.float32
BF16 = jnp.bfloat16


def adagrad(table_rows, accum_rows, grad_rows):
    new_accum = accum_rows + jnp.mean(grad_rows * grad_rows, axis=1)
    new_table = table_rows - 1.0 * grad_rows / (jnp.sqrt(new_accum)[:, None] + 1e-08)
    return (new_table, new_accum)


def general_body(
    table, accum, owner, local_row, lengths, queries, keys, cotangent, out_weight
):
    shards = lax.axis_size("shard")
    tok = owner.shape[0]
    rows_dev = table.shape[0]
    width = table.shape[1]
    heads = HEADS
    dqk = queries.shape[1] // heads
    dval = width // heads
    slots = 2 * tok // shards
    dest = owner[:, 0]
    onehot = (dest[:, None] == jnp.arange(shards)[None, :]).astype(jnp.bfloat16)
    pos = jnp.arange(tok)
    lower = (pos[None, :] < pos[:, None]).astype(jnp.bfloat16)
    before = jnp.dot(lower, onehot, preferred_element_type=jnp.float32)
    rank = jnp.sum(before * onehot.astype(jnp.float32), axis=1).astype(jnp.int32)
    slot = dest * slots + rank
    send_idx = (
        jnp.full((shards * slots,), -1, jnp.int32).at[slot].set(local_row).reshape(shards, slots)
    )
    recv_idx = lax.all_to_all(send_idx, "shard", split_axis=0, concat_axis=0, tiled=True).reshape(
        -1
    )
    valid = recv_idx >= 0
    picked = jnp.take(table, jnp.clip(recv_idx, 0, rows_dev - 1), axis=0)
    picked = (
        jnp.where(valid[:, None], picked, 0.0).astype(jnp.bfloat16).reshape(shards, slots, width)
    )
    ends = jnp.cumsum(lengths[0])
    seg = jnp.sum((pos[:, None] >= ends[None, :]).astype(jnp.int32), axis=1)
    mask = ((seg[:, None] == seg[None, :]) & (pos[None, :] <= pos[:, None])).astype(jnp.float32)
    q3 = queries.reshape(tok, heads, dqk)
    k3 = keys.reshape(tok, heads, dqk)
    scores = jnp.einsum("ihd,jhd->hij", q3, k3, preferred_element_type=jnp.float32) * dqk ** (-0.5)
    weights = (jax.nn.silu(scores) / MAXLEN * mask[None]).astype(jnp.bfloat16)
    fetched = lax.all_to_all(picked, "shard", split_axis=0, concat_axis=0, tiled=True).reshape(
        shards * slots, width
    )
    embedded = fetched[slot]
    vals = embedded.reshape(tok, heads, dval)
    mixed = (
        jnp.einsum("hij,jhd->ihd", weights, vals, preferred_element_type=jnp.float32)
        .reshape(tok, width)
        .astype(jnp.bfloat16)
    )
    back = lax.dot_general(
        cotangent,
        lax.all_gather(out_weight, "shard", axis=0, tiled=True),
        (((1,), (1,)), ((), ())),
        preferred_element_type=jnp.float32,
    ).astype(jnp.bfloat16)
    grad_share = lax.psum_scatter(
        lax.dot_general(
            mixed, cotangent, (((0,), (0,)), ((), ())), preferred_element_type=jnp.float32
        ),
        "shard",
        scatter_dimension=0,
        tiled=True,
    )
    weight_grad = lax.psum(grad_share, "replica").astype(jnp.bfloat16)
    b3 = back.reshape(tok, heads, dval)
    token_grad = jnp.einsum(
        "hij,ihd->jhd", weights, b3, preferred_element_type=jnp.float32
    ).reshape(tok, width)
    send_grad = (
        jnp.zeros((shards * slots, width), jnp.float32)
        .at[slot]
        .set(token_grad)
        .reshape(shards, slots, width)
    )
    arrived = (
        lax.all_to_all(
            send_grad.astype(jnp.bfloat16), "shard", split_axis=0, concat_axis=0, tiled=True
        )
        .astype(send_grad.dtype)
        .reshape(shards * slots, width)
    )
    select = (recv_idx[:, None] == jnp.arange(rows_dev)[None, :]).astype(jnp.float32)
    grad_rows = lax.dot_general(
        select,
        arrived,
        (((0,), (0,)), ((), ())),
        precision=lax.Precision.HIGHEST,
        preferred_element_type=jnp.float32,
    )
    share = lax.psum_scatter(
        grad_rows.astype(jnp.bfloat16), "replica", scatter_dimension=0, tiled=True
    ).astype(jnp.float32)
    quarter = share.shape[0]
    first = lax.axis_index("replica") * quarter
    part_table = lax.dynamic_slice_in_dim(table, first, quarter, 0)
    part_accum = lax.dynamic_slice_in_dim(accum, first, quarter, 0)
    upd_table, upd_accum = adagrad(part_table, part_accum, share)
    new_table, new_accum = (
        lax.all_gather(upd_table, "replica", axis=0, tiled=True),
        lax.all_gather(upd_accum, "replica", axis=0, tiled=True),
    )
    return (new_table, new_accum, weight_grad)


def iota(shape, axis):
    return lax.broadcasted_iota(jnp.int32, shape, axis)


def nt(a, b):
    return lax.dot_general(a, b, (((1,), (1,)), ((), ())), preferred_element_type=F32)


def nn(a, b):
    return lax.dot_general(a, b, (((1,), (0,)), ((), ())), preferred_element_type=F32)


def call(kernel, name, out, ins, smem=0, after=(), scratch=(), hbm=(), limit=32 << 20, cost=0, placed=False):
    n_in, n_after = len(ins), len(after)
    many = isinstance(out, (list, tuple))

    def run(*refs):
        refs = (*refs[:n_in], *refs[n_in + n_after :])
        if placed:
            shard = lax.axis_index("shard")
            kernel((lax.axis_index("replica"), shard // 2, shard % 2), *refs)
        else:
            kernel(*refs)

    return pl.pallas_call(
        run,
        out_shape=out,
        in_specs=[SMEM if i < smem else HBM if i in hbm else VMEM for i in range(n_in)]
        + [ANY] * n_after,
        out_specs=[VMEM] * len(out) if many else VMEM,
        scratch_shapes=list(scratch),
        name=name,
        cost_estimate=pl.CostEstimate(flops=cost, bytes_accessed=0, transcendentals=0),
        compiler_params=pltpu.CompilerParams(vmem_limit_bytes=limit),
    )(*ins, *after)


def sds(shape, dtype=BF16):
    return jax.ShapeDtypeStruct(shape, dtype)


def aligned(index, size):
    return pl.ds(pl.multiple_of(index * size, size), size)


def start_all(pairs, sem):
    copies = [pltpu.make_async_copy(a, b, sem.at[i]) for i, (a, b) in enumerate(pairs)]
    for c in copies:
        c.start()
    return copies


def pack_kernel(me, lens, owner, local, q, k, weight, table, out, out_z, rows_in, part_in, sem):
    n, _, pw = out.shape
    pw = pw // 2
    tok = q.shape[0]
    rows, cols = rows_in.shape
    part = part_in.shape[0]
    copies = start_all(
        [
            (table.at[:, aligned(me[0], cols)], rows_in),
            (weight.at[aligned(me[0], part), :], part_in),
        ]
        + [
            (x.at[:, i * pw : (i + 1) * pw], out.at[i, 0:tok, j * pw : (j + 1) * pw])
            for i in range(n)
            for j, x in enumerate((q, k))
        ],
        sem,
    )
    lane = iota((EXTRA, tok), 1)
    row = iota((EXTRA, tok), 0)
    seg = jnp.zeros((EXTRA, tok), F32)
    end = jnp.int32(0)
    for i in range(lens.shape[1]):
        end = end + lens[0, i]
        seg = seg + jnp.where(lane >= end, 1.0, 0.0)
    ids = jnp.where(
        row == 0,
        jnp.broadcast_to(owner[...].astype(F32), (EXTRA, tok)),
        jnp.where(
            row == 1,
            jnp.broadcast_to(local[...].astype(F32), (EXTRA, tok)),
            jnp.where(row == 2, seg, 0.0),
        ),
    ).astype(BF16)
    for i in range(n):
        out[i, tok : tok + EXTRA, :] = ids
    copies[0].wait()
    out_z[0:cols, :] = rows_in[...].T.astype(BF16)
    copies[1].wait()
    for i in range((out_z.shape[0] - cols) // part):
        out_z[cols + i * part : cols + (i + 1) * part, :] = part_in[:, i * rows : (i + 1) * rows]
    for c in copies[2:]:
        c.wait()


def pass_kernel(x, y, far_y, far_x, sem):
    half = far_x.shape[0]
    copies = start_all([(x.at[half:, :], far_y), (y.at[0:half, :], far_x)], sem)
    for c in copies:
        c.wait()


def stack_kernel(me, *refs):
    *blocks, out = refs
    cols = out.shape[1]
    for m, p in enumerate(blocks):
        out[me[1] ^ m] = p[0:cols, :]


def join_kernel(me, *refs):
    *parts, out = refs
    part = out.shape[0] // len(parts)
    rows = parts[0].shape[1]
    for m, p in enumerate(parts):
        for i in range(p.shape[0] // part):
            out[aligned(me[0] ^ m, part), i * rows : (i + 1) * rows] = p[i * part : (i + 1) * part, :]


def gate_kernel(out):
    out[...] = jnp.zeros_like(out)


def choose_kernel(me, *refs):
    n = (len(refs) - 1) // 2
    parts, out, held = refs[:n], refs[n : 2 * n], refs[2 * n]
    first = parts[0].shape[0] - held.shape[1]
    for m, p in enumerate(parts):
        held[m] = p[first:, :]
    for m, o in enumerate(out):
        o[...] = held[me[1] ^ me[0] ^ m]


def weights_kernel(me, packs, out):
    n, tok, pw = packs.shape
    tok, pw = tok - EXTRA, pw // 2
    heads = out.shape[1]
    dqk = pw // heads
    down, across = iota((tok, tok), 0), iota((tok, tok), 1)
    lane = iota((tok, pw), 1)
    for r in range(n):
        p = packs.at[me[0] ^ r]
        q = p[0:tok, 0:pw]
        k = p[0:tok, pw : 2 * pw]
        seg = ids_of(packs, me[0] ^ r)[2:3, :]
        seg_down = jnp.sum(jnp.where(down == across, seg, 0.0), axis=1, keepdims=True)
        mask = (seg == seg_down) & (down <= across)
        for j in range(heads):
            kj = jnp.where(lane // dqk == j, k, jnp.zeros_like(k))
            s = nt(kj, q) * dqk ** (-0.5)
            w = s / (1.0 + jnp.exp(-s)) * (1.0 / MAXLEN)
            out[r, j] = jnp.where(mask, w, 0.0).astype(BF16)


def ids_of(packs, r):
    rows = packs.shape[1]
    return packs[r, rows - EXTRA : rows, :].astype(F32)


def one_hot(ids, shard, rows):
    own, loc = ids[0:1, :], ids[1:2, :]
    named = jnp.where(own == shard.astype(F32), loc, -1.0)
    at = iota((rows, ids.shape[1]), 0).astype(F32)
    return jnp.where(at == named, 1.0, 0.0).astype(BF16)


def mix_kernel(me, packs, w, mine, other, out):
    n, cols, rows = mine.shape
    heads, tok = w.shape[1:3]
    dv = cols // heads
    blocks = jnp.concatenate([x[z] for z in range(n) for x in (mine, other)], axis=1)
    for r in range(n):
        ids = ids_of(packs, me[0] ^ r)
        picks = jnp.concatenate(
            [one_hot(ids, 2 * z + (me[2] ^ cc), rows) for z in range(n) for cc in range(2)], axis=0
        )
        vals = nn(blocks, picks).astype(BF16)
        for j in range(heads):
            out[j * dv : (j + 1) * dv, r * tok : (r + 1) * tok] = nn(
                vals[j * dv : (j + 1) * dv, :], w[r, j]
            ).astype(BF16)


def back_kernel(me, packs, ow_mine, ow_other, w, *refs):
    *cots, keep, send, ow, grad = refs
    n = packs.shape[0]
    heads, tok = w.shape[1:3]
    head_rows = ow_mine.shape[0]
    rows = send.shape[1]
    ow[aligned(me[2], head_rows), :] = ow_mine[...]
    ow[aligned(1 - me[2], head_rows), :] = ow_other[...]
    first = 0
    for cot in cots:
        end = first + cot.shape[0]
        grad[first:end, :] = nt(cot[...], ow[...]).astype(BF16)
        first = end
    for r in range(n):
        at_r = slice(r * tok, (r + 1) * tok)
        for j in range(heads):
            at_j = slice(j * head_rows, (j + 1) * head_rows)
            grad[at_r, at_j] = nn(w[r, j], grad[at_r, at_j]).astype(BF16)
    ids = jnp.concatenate([ids_of(packs, me[0] ^ r) for r in range(n)], axis=1)
    for cc in (1, 0):
        for z in range(n):
            total = nn(one_hot(ids, 2 * z + (me[2] ^ cc), rows), grad[...])
            if cc == 0:
                keep[z] = total
            else:
                send[z] = total.astype(BF16)


def wgrad_kernel(me, mixed, *refs):
    *cots, keep, send = refs
    rows = keep.shape[0]
    for cc, out in ((1, send), (0, keep)):
        at = aligned(me[2] ^ cc, rows)
        total = jnp.zeros(keep.shape, F32)
        first = 0
        for cot in cots:
            end = first + cot.shape[0]
            total = total + nn(mixed[at, first:end], cot[...])
            first = end
        out[...] = total.astype(out.dtype)


def add_kernel(keep, got, out):
    out[...] = (keep[...] + got[...].astype(F32)).astype(out.dtype)


def add_parts_kernel(me, keep, got, *out):
    rows = out[0].shape[0]
    for m, o in enumerate(out):
        at = aligned(me[0] ^ m, rows)
        o[...] = (keep[at, :] + got[at, :].astype(F32)).astype(o.dtype)


def sum_first_kernel(parts, out):
    total = parts[0].astype(F32)
    for m in range(1, parts.shape[0]):
        total = total + parts[m].astype(F32)
    out[...] = total.astype(out.dtype)


def sum_kernel(*refs):
    *parts, out = refs
    total = parts[0][...].astype(F32)
    for p in parts[1:]:
        total = total + p[...].astype(F32)
    out[...] = total.astype(out.dtype)


def place_kernel(me, *refs):
    *parts, out = refs
    rows = parts[0].shape[0]
    for m, p in enumerate(parts):
        out[aligned(me[0] ^ m, rows), :] = p[...]


def update_kernel(me, table, accum, *refs):
    *parts, new_table, new_accum, grad = refs
    rows, width = table.shape
    cols = width // len(parts)
    for m, p in enumerate(parts):
        grad[:, aligned(me[0] ^ m, cols)] = p[...].astype(F32)
    mean = jnp.sum(grad[...] * grad[...], axis=1, keepdims=True) * (1.0 / width)
    same = iota((rows, rows), 0) == iota((rows, rows), 1)
    old = jnp.sum(jnp.where(same, accum[...], 0.0), axis=1, keepdims=True)
    fresh = old + mean
    new_accum[...] = jnp.sum(jnp.where(same, fresh, 0.0), axis=0, keepdims=True)
    new_table[...] = table[...] - grad[...] / (jnp.sqrt(fresh) + 1e-08)


def body(table, accum, owner, local_row, lengths, queries, keys, cotangent, out_weight):
    n = lax.axis_size("replica")
    shards = lax.axis_size("shard")
    tok = owner.shape[0]
    rows, width = table.shape
    cols = width // n
    heads = HEADS // n
    part = out_weight.shape[0] // n

    def column(x, m):
        return lax.ppermute(x, "replica", [(i, i ^ m) for i in range(n)]) if m else x

    def along(x, m):
        return lax.ppermute(x, "shard", [(i, i ^ (2 * m)) for i in range(shards)]) if m else x

    def core(x):
        return lax.ppermute(x, "shard", [(i, i ^ 1) for i in range(shards)])

    def swap_along(x):
        groups = [list(range(c, shards, 2)) for c in range(2)]
        return lax.all_to_all(x, "shard", 0, 0, tiled=True, axis_index_groups=groups)

    def swap_columns(x):
        return lax.all_to_all(x, "replica", 0, 0, tiled=True)

    half = tok // 2
    x, y = column(cotangent, 1), column(cotangent, 2)
    zrows = cols + part * width // rows
    packs, zpay = call(
        pack_kernel,
        "pack",
        [sds((n, tok + EXTRA, 2 * queries.shape[1] // n)), sds((zrows, rows))],
        (
            lengths,
            owner.reshape(1, tok),
            local_row.reshape(1, tok),
            queries,
            keys,
            out_weight,
            table,
        ),
        smem=1,
        hbm=(3, 4, 5, 6),
        scratch=[
            pltpu.VMEM((rows, cols), F32),
            pltpu.VMEM((part, width), BF16),
            pltpu.SemaphoreType.DMA((2 * n + 2,)),
        ],
        limit=None,
        placed=True,
    )
    packs = swap_columns(packs)
    blocks = [along(zpay, m) for m in range(n)]
    far_y, far_x = call(
        pass_kernel,
        "pass",
        [sds((half, width))] * 2,
        (x, y),
        scratch=[pltpu.SemaphoreType.DMA((2,))],
        cost=PASS_COST,
    )
    w = call(
        weights_kernel,
        "weights",
        sds((n, heads, tok, tok)),
        (packs,),
        after=(far_x,),
        placed=True,
    )
    owp = call(
        choose_kernel,
        "choose",
        [sds((zrows - cols, rows))] * n,
        blocks,
        after=(w,),
        scratch=[pltpu.VMEM((n, zrows - cols, rows), BF16)],
        placed=True,
    )
    mine = call(
        stack_kernel, "stack", sds((n, cols, rows)), blocks, after=(owp[0],), placed=True
    )
    other = core(mine)
    owp = [column(p, m) for m, p in enumerate(owp)]
    ow_mine = call(join_kernel, "join", sds((n * part, width)), owp, placed=True)
    ow_other = core(ow_mine)
    far_y, far_x = column(far_y, 2), column(far_x, 1)
    cots = [cotangent, x, y, far_x, far_y]
    here = call(gate_kernel, "gate", sds((8, 128), F32), (), after=(far_x, far_y), cost=GATE_COST)

    mixed = call(
        mix_kernel, "mix", sds((cols, n * tok)), (packs, w, mine, other), placed=True
    )
    keep, send = call(
        back_kernel,
        "back",
        [sds((n, rows, cols), F32), sds((n, rows, cols))],
        (packs, ow_mine, ow_other, w, *cots),
        after=(here, mixed),
        scratch=[pltpu.VMEM((cols, width), BF16), pltpu.VMEM((n * tok, cols), BF16)],
        placed=True,
    )
    sums = call(add_kernel, "add", sds((n, rows, cols)), (keep, core(send)))
    ready = sums
    sums = swap_along(sums)
    wkeep, wsend = call(
        wgrad_kernel,
        "wgrad",
        [sds((n * part, width), F32), sds((n * part, width))],
        (mixed, *cots),
        after=(ready,),
        placed=True,
    )
    wgot = core(wsend)

    wparts = call(
        add_parts_kernel, "add_parts", [sds((part, width))] * n, (wkeep, wgot), placed=True
    )
    wparts = [column(p, m) for m, p in enumerate(wparts)]
    wparts = call(
        choose_kernel,
        "pick",
        [sds((part, width))] * n,
        wparts,
        placed=True,
        scratch=[pltpu.VMEM((n, part, width), BF16)],
    )
    wready = wparts[0]
    wparts = [along(p, m) for m, p in enumerate(wparts)]

    grad = call(sum_first_kernel, "sum_rows", sds((rows, cols)), (sums,), after=(wready,))
    grads = [column(grad, m) for m in range(n)]
    wsum = call(sum_kernel, "sum_parts", sds((part, width)), wparts, after=(grads[1],))
    wsums = [column(wsum, m) for m in range(n)]
    new_table, new_accum = call(
        update_kernel,
        "update",
        [sds((rows, width), F32), sds((1, rows), F32)],
        (table, accum.reshape(1, rows), *grads),
        placed=True,
        scratch=[pltpu.VMEM((rows, width), F32)],
    )
    weight_grad = call(place_kernel, "place", sds((n * part, width)), wsums, placed=True)
    return (new_table, new_accum.reshape(rows), weight_grad)


def fits(mesh):
    n, shards = mesh.shape["replica"], mesh.shape["shard"]
    return n & (n - 1) == 0 and shards == HEADS and 2 * n == HEADS


def solution(mesh):
    placed = (
        P("shard", None),
        P("shard"),
        P(("replica", "shard"), None),
        P(("replica", "shard")),
        P(("replica", "shard"), None),
        P(("replica", "shard"), None),
        P(("replica", "shard"), None),
        P(("replica", "shard"), None),
        P("shard", None),
    )
    return jax.shard_map(
        body if fits(mesh) else general_body,
        mesh=mesh,
        in_specs=placed,
        out_specs=(P("shard", None), P("shard"), P("shard", None)),
        check_vma=False,
    )
```

```python
import functools

import jax
import jax.numpy as jnp
from jax import lax
from jax.experimental import pallas as pl
from jax.experimental.pallas import tpu as pltpu
from jax.sharding import PartitionSpec as P

HEADS = 8
MAXLEN = 128
PASS_COST = 12 * 10**9
GATE_COST = 8 * 10**9
EXTRA = 16
VMEM = pl.BlockSpec(memory_space=pltpu.VMEM)
ANY = pl.BlockSpec(memory_space=pl.ANY)
HBM = pl.BlockSpec(memory_space=pltpu.HBM)
SMEM = pl.BlockSpec(memory_space=pltpu.SMEM)
F32 = jnp.float32
BF16 = jnp.bfloat16


def adagrad(table_rows, accum_rows, grad_rows):
    new_accum = accum_rows + jnp.mean(grad_rows * grad_rows, axis=1)
    new_table = table_rows - 1.0 * grad_rows / (jnp.sqrt(new_accum)[:, None] + 1e-08)
    return (new_table, new_accum)


def general_body(
    table, accum, owner, local_row, lengths, queries, keys, cotangent, out_weight
):
    shards = lax.axis_size("shard")
    tok = owner.shape[0]
    rows_dev = table.shape[0]
    width = table.shape[1]
    heads = HEADS
    dqk = queries.shape[1] // heads
    dval = width // heads
    slots = 2 * tok // shards
    dest = owner[:, 0]
    onehot = (dest[:, None] == jnp.arange(shards)[None, :]).astype(jnp.bfloat16)
    pos = jnp.arange(tok)
    lower = (pos[None, :] < pos[:, None]).astype(jnp.bfloat16)
    before = jnp.dot(lower, onehot, preferred_element_type=jnp.float32)
    rank = jnp.sum(before * onehot.astype(jnp.float32), axis=1).astype(jnp.int32)
    slot = dest * slots + rank
    send_idx = (
        jnp.full((shards * slots,), -1, jnp.int32).at[slot].set(local_row).reshape(shards, slots)
    )
    recv_idx = lax.all_to_all(send_idx, "shard", split_axis=0, concat_axis=0, tiled=True).reshape(
        -1
    )
    valid = recv_idx >= 0
    picked = jnp.take(table, jnp.clip(recv_idx, 0, rows_dev - 1), axis=0)
    picked = (
        jnp.where(valid[:, None], picked, 0.0).astype(jnp.bfloat16).reshape(shards, slots, width)
    )
    ends = jnp.cumsum(lengths[0])
    seg = jnp.sum((pos[:, None] >= ends[None, :]).astype(jnp.int32), axis=1)
    mask = ((seg[:, None] == seg[None, :]) & (pos[None, :] <= pos[:, None])).astype(jnp.float32)
    q3 = queries.reshape(tok, heads, dqk)
    k3 = keys.reshape(tok, heads, dqk)
    scores = jnp.einsum("ihd,jhd->hij", q3, k3, preferred_element_type=jnp.float32) * dqk ** (-0.5)
    weights = (jax.nn.silu(scores) / MAXLEN * mask[None]).astype(jnp.bfloat16)
    fetched = lax.all_to_all(picked, "shard", split_axis=0, concat_axis=0, tiled=True).reshape(
        shards * slots, width
    )
    embedded = fetched[slot]
    vals = embedded.reshape(tok, heads, dval)
    mixed = (
        jnp.einsum("hij,jhd->ihd", weights, vals, preferred_element_type=jnp.float32)
        .reshape(tok, width)
        .astype(jnp.bfloat16)
    )
    back = lax.dot_general(
        cotangent,
        lax.all_gather(out_weight, "shard", axis=0, tiled=True),
        (((1,), (1,)), ((), ())),
        preferred_element_type=jnp.float32,
    ).astype(jnp.bfloat16)
    grad_share = lax.psum_scatter(
        lax.dot_general(
            mixed, cotangent, (((0,), (0,)), ((), ())), preferred_element_type=jnp.float32
        ),
        "shard",
        scatter_dimension=0,
        tiled=True,
    )
    weight_grad = lax.psum(grad_share, "replica").astype(jnp.bfloat16)
    b3 = back.reshape(tok, heads, dval)
    token_grad = jnp.einsum(
        "hij,ihd->jhd", weights, b3, preferred_element_type=jnp.float32
    ).reshape(tok, width)
    send_grad = (
        jnp.zeros((shards * slots, width), jnp.float32)
        .at[slot]
        .set(token_grad)
        .reshape(shards, slots, width)
    )
    arrived = (
        lax.all_to_all(
            send_grad.astype(jnp.bfloat16), "shard", split_axis=0, concat_axis=0, tiled=True
        )
        .astype(send_grad.dtype)
        .reshape(shards * slots, width)
    )
    select = (recv_idx[:, None] == jnp.arange(rows_dev)[None, :]).astype(jnp.float32)
    grad_rows = lax.dot_general(
        select,
        arrived,
        (((0,), (0,)), ((), ())),
        precision=lax.Precision.HIGHEST,
        preferred_element_type=jnp.float32,
    )
    share = lax.psum_scatter(
        grad_rows.astype(jnp.bfloat16), "replica", scatter_dimension=0, tiled=True
    ).astype(jnp.float32)
    quarter = share.shape[0]
    first = lax.axis_index("replica") * quarter
    part_table = lax.dynamic_slice_in_dim(table, first, quarter, 0)
    part_accum = lax.dynamic_slice_in_dim(accum, first, quarter, 0)
    upd_table, upd_accum = adagrad(part_table, part_accum, share)
    new_table, new_accum = (
        lax.all_gather(upd_table, "replica", axis=0, tiled=True),
        lax.all_gather(upd_accum, "replica", axis=0, tiled=True),
    )
    return (new_table, new_accum, weight_grad)


def iota(shape, axis):
    return lax.broadcasted_iota(jnp.int32, shape, axis)


def nt(a, b):
    return lax.dot_general(a, b, (((1,), (1,)), ((), ())), preferred_element_type=F32)


def nn(a, b):
    return lax.dot_general(a, b, (((1,), (0,)), ((), ())), preferred_element_type=F32)


def call(
    kernel,
    name,
    out,
    ins,
    smem=0,
    after=(),
    scratch=(),
    hbm=(),
    limit=16 << 20,
    cost=0,
    placed=False,
    out_hbm=False,
):
    n_in, n_after = len(ins), len(after)
    many = isinstance(out, (list, tuple))

    def run(*refs):
        refs = (*refs[:n_in], *refs[n_in + n_after :])
        if placed:
            shard = lax.axis_index("shard")
            kernel((lax.axis_index("replica"), shard // 2, shard % 2), *refs)
        else:
            kernel(*refs)

    return pl.pallas_call(
        run,
        out_shape=out,
        in_specs=[SMEM if i < smem else HBM if i in hbm else VMEM for i in range(n_in)]
        + [ANY] * n_after,
        out_specs=HBM if out_hbm else [VMEM] * len(out) if many else VMEM,
        scratch_shapes=list(scratch),
        name=name,
        cost_estimate=pl.CostEstimate(flops=cost, bytes_accessed=0, transcendentals=0),
        compiler_params=pltpu.CompilerParams(vmem_limit_bytes=limit),
    )(*ins, *after)


def sds(shape, dtype=BF16):
    return jax.ShapeDtypeStruct(shape, dtype)


def aligned(index, size):
    return pl.ds(pl.multiple_of(index * size, size), size)


def start_all(pairs, sem):
    copies = [pltpu.make_async_copy(a, b, sem.at[i]) for i, (a, b) in enumerate(pairs)]
    for c in copies:
        c.start()
    return copies


def carry_kernel(me, weight, table, out, rows_in, part_in, sem):
    rows, cols = rows_in.shape
    part = part_in.shape[0]
    copies = start_all(
        [
            (table.at[:, aligned(me[0], cols)], rows_in),
            (weight.at[aligned(me[0], part), :], part_in),
        ],
        sem,
    )
    copies[1].wait()
    for i in range((out.shape[0] - cols) // part):
        out[cols + i * part : cols + (i + 1) * part, :] = part_in[:, i * rows : (i + 1) * rows]
    copies[0].wait()
    out[0:cols, :] = rows_in[...].T.astype(BF16)


def pack_kernel(lens, owner, local, q, k, out, ids, sem):
    n, rows, pw = out.shape
    tok = q.shape[0]
    runs = tok // pw
    later = start_all(
        [
            (x.at[:, i * pw : (i + 1) * pw], out.at[i, j * tok : (j + 1) * tok, :])
            for i in range(n)
            for j, x in enumerate((q, k))
        ],
        sem,
    )
    lane = iota((EXTRA, tok), 1)
    row = iota((EXTRA, tok), 0)
    seg = jnp.zeros((EXTRA, tok), F32)
    end = jnp.int32(0)
    for i in range(lens.shape[1]):
        end = end + lens[0, i]
        seg = seg + jnp.where(lane >= end, 1.0, 0.0)
    all_ids = jnp.where(
        row == 0,
        jnp.broadcast_to(owner[...].astype(F32), (EXTRA, tok)),
        jnp.where(
            row == 1,
            jnp.broadcast_to(local[...].astype(F32), (EXTRA, tok)),
            jnp.where(row == 2, seg, 0.0),
        ),
    ).astype(BF16)
    for i in range(runs):
        ids[i * EXTRA : (i + 1) * EXTRA, :] = all_ids[:, i * pw : (i + 1) * pw]
    later = later + start_all(
        [(ids, out.at[i, 2 * tok : rows, :]) for i in range(n)], sem.at[pl.ds(2 * n, n)]
    )
    for c in later:
        c.wait()


def pass_kernel(x, y, far_y, far_x, sem):
    half = far_x.shape[0]
    copies = start_all([(x.at[half:, :], far_y), (y.at[0:half, :], far_x)], sem)
    for c in copies:
        c.wait()


def stack_kernel(me, *refs):
    *blocks, out = refs
    cols = out.shape[1]
    for m, p in enumerate(blocks):
        out[me[1] ^ m] = p[0:cols, :]


def join_kernel(me, *refs):
    *parts, out = refs
    part = out.shape[0] // len(parts)
    rows = parts[0].shape[1]
    for m, p in enumerate(parts):
        for i in range(p.shape[0] // part):
            out[aligned(me[0] ^ m, part), i * rows : (i + 1) * rows] = p[i * part : (i + 1) * part, :]


def gate_kernel(out):
    out[...] = jnp.zeros_like(out)


def choose_kernel(me, *refs):
    n = (len(refs) - 1) // 2
    parts, out, held = refs[:n], refs[n : 2 * n], refs[2 * n]
    first = parts[0].shape[0] - held.shape[1]
    for m, p in enumerate(parts):
        held[m] = p[first:, :]
    for m, o in enumerate(out):
        o[...] = held[me[1] ^ me[0] ^ m]


def weights_kernel(me, packs, out):
    n, _, pw = packs.shape
    heads, tok = out.shape[1:3]
    dqk = pw // heads
    down, across = iota((tok, tok), 0), iota((tok, tok), 1)
    lane = iota((tok, pw), 1)
    for r in range(n):
        p = packs.at[me[0] ^ r]
        q = p[0:tok, :]
        k = p[tok : 2 * tok, :]
        seg = ids_of(packs, me[0] ^ r, tok)[2:3, :]
        seg_down = jnp.sum(jnp.where(down == across, seg, 0.0), axis=1, keepdims=True)
        mask = (seg == seg_down) & (down <= across)
        for j in range(heads):
            kj = jnp.where(lane // dqk == j, k, jnp.zeros_like(k))
            s = nt(kj, q) * dqk ** (-0.5)
            w = s / (1.0 + jnp.exp(-s)) * (1.0 / MAXLEN)
            out[r, j] = jnp.where(mask, w, 0.0).astype(BF16)


def ids_of(packs, r, tok):
    runs = tok // packs.shape[2]
    ids = packs[r, 2 * tok : 2 * tok + runs * EXTRA, :].astype(F32)
    return jnp.concatenate([ids[i * EXTRA : (i + 1) * EXTRA] for i in range(runs)], axis=1)


def one_hot(ids, shard, rows):
    own, loc = ids[0:1, :], ids[1:2, :]
    named = jnp.where(own == shard.astype(F32), loc, -1.0)
    at = iota((rows, ids.shape[1]), 0).astype(F32)
    return jnp.where(at == named, 1.0, 0.0).astype(BF16)


def mix_kernel(me, packs, w, mine, other, out):
    n, cols, rows = mine.shape
    heads, tok = w.shape[1:3]
    dv = cols // heads
    blocks = jnp.concatenate([x[z] for z in range(n) for x in (mine, other)], axis=1)
    for r in range(n):
        ids = ids_of(packs, me[0] ^ r, w.shape[2])
        picks = jnp.concatenate(
            [one_hot(ids, 2 * z + (me[2] ^ cc), rows) for z in range(n) for cc in range(2)], axis=0
        )
        vals = nn(blocks, picks).astype(BF16)
        for j in range(heads):
            out[j * dv : (j + 1) * dv, r * tok : (r + 1) * tok] = nn(
                vals[j * dv : (j + 1) * dv, :], w[r, j]
            ).astype(BF16)


def by_row(me, packs, grad, core, z, rows):
    n = packs.shape[0]
    tok = grad.shape[0] // n
    ids = jnp.concatenate([ids_of(packs, me[0] ^ r, tok) for r in range(n)], axis=1)
    return nn(one_hot(ids, 2 * z + core, rows), grad[...])


def back_kernel(me, packs, ow_mine, ow_other, w, *refs):
    *cots, send, grad, ow = refs
    n = packs.shape[0]
    heads, tok = w.shape[1:3]
    head_rows = ow_mine.shape[0]
    ow[aligned(me[2], head_rows), :] = ow_mine[...]
    ow[aligned(1 - me[2], head_rows), :] = ow_other[...]
    first = 0
    for cot in cots:
        end = first + cot.shape[0]
        grad[first:end, :] = nt(cot[...], ow[...]).astype(BF16)
        first = end
    for r in range(n):
        at_r = slice(r * tok, (r + 1) * tok)
        for j in range(heads):
            at_j = slice(j * head_rows, (j + 1) * head_rows)
            grad[at_r, at_j] = nn(w[r, j], grad[at_r, at_j]).astype(BF16)
    for z in range(n):
        send[z] = by_row(me, packs, grad, 1 - me[2], z, send.shape[1]).astype(BF16)


def keep_kernel(me, packs, grad, keep):
    for z in range(keep.shape[0]):
        keep[z] = by_row(me, packs, grad, me[2], z, keep.shape[1])


def wgrad_kernel(me, mixed, *refs):
    *cots, keep, send = refs
    rows = keep.shape[0]
    for cc, out in ((1, send), (0, keep)):
        at = aligned(me[2] ^ cc, rows)
        total = jnp.zeros(keep.shape, F32)
        first = 0
        for cot in cots:
            end = first + cot.shape[0]
            total = total + nn(mixed[at, first:end], cot[...])
            first = end
        out[...] = total.astype(out.dtype)


def add_kernel(keep, got, out):
    out[...] = (keep[...] + got[...].astype(F32)).astype(out.dtype)


def add_parts_kernel(me, keep, got, *out):
    rows = out[0].shape[0]
    for m, o in enumerate(out):
        at = aligned(me[0] ^ m, rows)
        o[...] = (keep[at, :] + got[at, :].astype(F32)).astype(o.dtype)


def sum_first_kernel(parts, out):
    total = parts[0].astype(F32)
    for m in range(1, parts.shape[0]):
        total = total + parts[m].astype(F32)
    out[...] = total.astype(out.dtype)


def sum_kernel(*refs):
    *parts, out = refs
    total = parts[0][...].astype(F32)
    for p in parts[1:]:
        total = total + p[...].astype(F32)
    out[...] = total.astype(out.dtype)


def place_kernel(me, *refs):
    *parts, out = refs
    rows = parts[0].shape[0]
    for m, p in enumerate(parts):
        out[aligned(me[0] ^ m, rows), :] = p[...]


def update_kernel(me, table, accum, *refs):
    *parts, new_table, new_accum, grad = refs
    rows, width = table.shape
    cols = width // len(parts)
    for m, p in enumerate(parts):
        grad[:, aligned(me[0] ^ m, cols)] = p[...].astype(F32)
    mean = jnp.sum(grad[...] * grad[...], axis=1, keepdims=True) * (1.0 / width)
    same = iota((rows, rows), 0) == iota((rows, rows), 1)
    old = jnp.sum(jnp.where(same, accum[...], 0.0), axis=1, keepdims=True)
    fresh = old + mean
    new_accum[...] = jnp.sum(jnp.where(same, fresh, 0.0), axis=0, keepdims=True)
    new_table[...] = table[...] - grad[...] / (jnp.sqrt(fresh) + 1e-08)


def body(table, accum, owner, local_row, lengths, queries, keys, cotangent, out_weight):
    n = lax.axis_size("replica")
    shards = lax.axis_size("shard")
    tok = owner.shape[0]
    rows, width = table.shape
    cols = width // n
    heads = HEADS // n
    part = out_weight.shape[0] // n

    def column(x, m):
        return lax.ppermute(x, "replica", [(i, i ^ m) for i in range(n)]) if m else x

    def along(x, m):
        return lax.ppermute(x, "shard", [(i, i ^ (2 * m)) for i in range(shards)]) if m else x

    def core(x):
        return lax.ppermute(x, "shard", [(i, i ^ 1) for i in range(shards)])

    def swap_along(x):
        groups = [list(range(c, shards, 2)) for c in range(2)]
        return lax.all_to_all(x, "shard", 0, 0, tiled=True, axis_index_groups=groups)

    def swap_columns(x):
        return lax.all_to_all(x, "replica", 0, 0, tiled=True)

    half = tok // 2
    x, y = column(cotangent, 1), column(cotangent, 2)
    zrows = cols + part * width // rows
    zpay = call(
        carry_kernel,
        "carry",
        sds((zrows, rows)),
        (out_weight, table),
        hbm=(0, 1),
        scratch=[
            pltpu.VMEM((rows, cols), F32),
            pltpu.VMEM((part, width), BF16),
            pltpu.SemaphoreType.DMA((2,)),
        ],
        limit=None,
        placed=True,
    )
    pw = queries.shape[1] // n
    packs = call(
        pack_kernel,
        "pack",
        sds((n, 2 * tok + tok // pw * EXTRA, pw)),
        (lengths, owner.reshape(1, tok), local_row.reshape(1, tok), queries, keys),
        smem=1,
        out_hbm=True,
        scratch=[
            pltpu.VMEM((tok // pw * EXTRA, pw), BF16),
            pltpu.SemaphoreType.DMA((3 * n,)),
        ],
    )
    packs = swap_columns(packs)
    blocks = [along(zpay, m) for m in range(n)]
    far_y, far_x = call(
        pass_kernel,
        "pass",
        [sds((half, width))] * 2,
        (x, y),
        scratch=[pltpu.SemaphoreType.DMA((2,))],
        cost=PASS_COST,
    )
    w = call(
        weights_kernel,
        "weights",
        sds((n, heads, tok, tok)),
        (packs,),
        after=(far_x,),
        placed=True,
    )
    owp = call(
        choose_kernel,
        "choose",
        [sds((zrows - cols, rows))] * n,
        blocks,
        after=(packs,),
        scratch=[pltpu.VMEM((n, zrows - cols, rows), BF16)],
        placed=True,
    )
    mine = call(
        stack_kernel, "stack", sds((n, cols, rows)), blocks, after=(owp[0],), placed=True
    )
    other = core(mine)
    owp = [column(p, m) for m, p in enumerate(owp)]
    ow_mine = call(join_kernel, "join", sds((n * part, width)), owp, placed=True)
    ow_other = core(ow_mine)
    far_y, far_x = column(far_y, 2), column(far_x, 1)
    cots = [cotangent, x, y, far_x, far_y]
    here = call(gate_kernel, "gate", sds((8, 128), F32), (), after=(far_x, far_y), cost=GATE_COST)

    mixed = call(
        mix_kernel, "mix", sds((cols, n * tok)), (packs, w, mine, other), placed=True
    )
    send, grad = call(
        back_kernel,
        "back",
        [sds((n, rows, cols)), sds((n * tok, cols))],
        (packs, ow_mine, ow_other, w, *cots),
        after=(here, mixed),
        scratch=[pltpu.VMEM((cols, width), BF16)],
        placed=True,
    )
    got = core(send)
    keep = call(keep_kernel, "keep", sds((n, rows, cols), F32), (packs, grad), placed=True)
    sums = call(add_kernel, "add", sds((n, rows, cols)), (keep, got))
    ready = sums
    sums = swap_along(sums)
    wkeep, wsend = call(
        wgrad_kernel,
        "wgrad",
        [sds((n * part, width), F32), sds((n * part, width))],
        (mixed, *cots),
        after=(ready,),
        placed=True,
    )
    wgot = core(wsend)

    wparts = call(
        add_parts_kernel, "add_parts", [sds((part, width))] * n, (wkeep, wgot), placed=True
    )
    wparts = [column(p, m) for m, p in enumerate(wparts)]
    wparts = call(
        choose_kernel,
        "pick",
        [sds((part, width))] * n,
        wparts,
        placed=True,
        scratch=[pltpu.VMEM((n, part, width), BF16)],
    )
    wparts = [along(p, m) for m, p in enumerate(wparts)]

    grad = call(sum_first_kernel, "sum_rows", sds((rows, cols)), (sums,))
    grads = [column(grad, m) for m in range(n)]
    wsum = call(sum_kernel, "sum_parts", sds((part, width)), wparts, after=(grads[1],))
    wsums = [column(wsum, m) for m in range(n)]
    new_table, new_accum = call(
        update_kernel,
        "update",
        [sds((rows, width), F32), sds((1, rows), F32)],
        (table, accum.reshape(1, rows), *grads),
        placed=True,
        scratch=[pltpu.VMEM((rows, width), F32)],
    )
    weight_grad = call(place_kernel, "place", sds((n * part, width)), wsums, placed=True)
    return (new_table, new_accum.reshape(rows), weight_grad)


def fits(mesh):
    n, shards = mesh.shape["replica"], mesh.shape["shard"]
    return n & (n - 1) == 0 and shards == HEADS and 2 * n == HEADS


def solution(mesh):
    placed = (
        P("shard", None),
        P("shard"),
        P(("replica", "shard"), None),
        P(("replica", "shard")),
        P(("replica", "shard"), None),
        P(("replica", "shard"), None),
        P(("replica", "shard"), None),
        P(("replica", "shard"), None),
        P("shard", None),
    )
    return jax.shard_map(
        body if fits(mesh) else general_body,
        mesh=mesh,
        in_specs=placed,
        out_specs=(P("shard", None), P("shard"), P("shard", None)),
        check_vma=False,
    )
```

```python
import functools

import jax
import jax.numpy as jnp
from jax import lax
from jax.experimental import pallas as pl
from jax.experimental.pallas import tpu as pltpu
from jax.sharding import PartitionSpec as P

HEADS = 8
MAXLEN = 128
PASS_COST = 12 * 10**9
PARTS_COST = 4 * 10**9
UPDATE_COST = 8 * 10**9
GATE_COST = 8 * 10**9
EXTRA = 16
VMEM = pl.BlockSpec(memory_space=pltpu.VMEM)
ANY = pl.BlockSpec(memory_space=pl.ANY)
HBM = pl.BlockSpec(memory_space=pltpu.HBM)
SMEM = pl.BlockSpec(memory_space=pltpu.SMEM)
F32 = jnp.float32
BF16 = jnp.bfloat16


def adagrad(table_rows, accum_rows, grad_rows):
    new_accum = accum_rows + jnp.mean(grad_rows * grad_rows, axis=1)
    new_table = table_rows - 1.0 * grad_rows / (jnp.sqrt(new_accum)[:, None] + 1e-08)
    return (new_table, new_accum)


def general_body(
    table, accum, owner, local_row, lengths, queries, keys, cotangent, out_weight
):
    shards = lax.axis_size("shard")
    tok = owner.shape[0]
    rows_dev = table.shape[0]
    width = table.shape[1]
    heads = HEADS
    dqk = queries.shape[1] // heads
    dval = width // heads
    slots = 2 * tok // shards
    dest = owner[:, 0]
    onehot = (dest[:, None] == jnp.arange(shards)[None, :]).astype(jnp.bfloat16)
    pos = jnp.arange(tok)
    lower = (pos[None, :] < pos[:, None]).astype(jnp.bfloat16)
    before = jnp.dot(lower, onehot, preferred_element_type=jnp.float32)
    rank = jnp.sum(before * onehot.astype(jnp.float32), axis=1).astype(jnp.int32)
    slot = dest * slots + rank
    send_idx = (
        jnp.full((shards * slots,), -1, jnp.int32).at[slot].set(local_row).reshape(shards, slots)
    )
    recv_idx = lax.all_to_all(send_idx, "shard", split_axis=0, concat_axis=0, tiled=True).reshape(
        -1
    )
    valid = recv_idx >= 0
    picked = jnp.take(table, jnp.clip(recv_idx, 0, rows_dev - 1), axis=0)
    picked = (
        jnp.where(valid[:, None], picked, 0.0).astype(jnp.bfloat16).reshape(shards, slots, width)
    )
    ends = jnp.cumsum(lengths[0])
    seg = jnp.sum((pos[:, None] >= ends[None, :]).astype(jnp.int32), axis=1)
    mask = ((seg[:, None] == seg[None, :]) & (pos[None, :] <= pos[:, None])).astype(jnp.float32)
    q3 = queries.reshape(tok, heads, dqk)
    k3 = keys.reshape(tok, heads, dqk)
    scores = jnp.einsum("ihd,jhd->hij", q3, k3, preferred_element_type=jnp.float32) * dqk ** (-0.5)
    weights = (jax.nn.silu(scores) / MAXLEN * mask[None]).astype(jnp.bfloat16)
    fetched = lax.all_to_all(picked, "shard", split_axis=0, concat_axis=0, tiled=True).reshape(
        shards * slots, width
    )
    embedded = fetched[slot]
    vals = embedded.reshape(tok, heads, dval)
    mixed = (
        jnp.einsum("hij,jhd->ihd", weights, vals, preferred_element_type=jnp.float32)
        .reshape(tok, width)
        .astype(jnp.bfloat16)
    )
    back = lax.dot_general(
        cotangent,
        lax.all_gather(out_weight, "shard", axis=0, tiled=True),
        (((1,), (1,)), ((), ())),
        preferred_element_type=jnp.float32,
    ).astype(jnp.bfloat16)
    grad_share = lax.psum_scatter(
        lax.dot_general(
            mixed, cotangent, (((0,), (0,)), ((), ())), preferred_element_type=jnp.float32
        ),
        "shard",
        scatter_dimension=0,
        tiled=True,
    )
    weight_grad = lax.psum(grad_share, "replica").astype(jnp.bfloat16)
    b3 = back.reshape(tok, heads, dval)
    token_grad = jnp.einsum(
        "hij,ihd->jhd", weights, b3, preferred_element_type=jnp.float32
    ).reshape(tok, width)
    send_grad = (
        jnp.zeros((shards * slots, width), jnp.float32)
        .at[slot]
        .set(token_grad)
        .reshape(shards, slots, width)
    )
    arrived = (
        lax.all_to_all(
            send_grad.astype(jnp.bfloat16), "shard", split_axis=0, concat_axis=0, tiled=True
        )
        .astype(send_grad.dtype)
        .reshape(shards * slots, width)
    )
    select = (recv_idx[:, None] == jnp.arange(rows_dev)[None, :]).astype(jnp.float32)
    grad_rows = lax.dot_general(
        select,
        arrived,
        (((0,), (0,)), ((), ())),
        precision=lax.Precision.HIGHEST,
        preferred_element_type=jnp.float32,
    )
    share = lax.psum_scatter(
        grad_rows.astype(jnp.bfloat16), "replica", scatter_dimension=0, tiled=True
    ).astype(jnp.float32)
    quarter = share.shape[0]
    first = lax.axis_index("replica") * quarter
    part_table = lax.dynamic_slice_in_dim(table, first, quarter, 0)
    part_accum = lax.dynamic_slice_in_dim(accum, first, quarter, 0)
    upd_table, upd_accum = adagrad(part_table, part_accum, share)
    new_table, new_accum = (
        lax.all_gather(upd_table, "replica", axis=0, tiled=True),
        lax.all_gather(upd_accum, "replica", axis=0, tiled=True),
    )
    return (new_table, new_accum, weight_grad)


def iota(shape, axis):
    return lax.broadcasted_iota(jnp.int32, shape, axis)


def nt(a, b):
    return lax.dot_general(a, b, (((1,), (1,)), ((), ())), preferred_element_type=F32)


def nn(a, b):
    return lax.dot_general(a, b, (((1,), (0,)), ((), ())), preferred_element_type=F32)


def call(
    kernel,
    name,
    out,
    ins,
    smem=0,
    after=(),
    scratch=(),
    hbm=(),
    limit=16 << 20,
    cost=0,
    placed=False,
    out_hbm=False,
):
    n_in, n_after = len(ins), len(after)
    many = isinstance(out, (list, tuple))

    def run(*refs):
        refs = (*refs[:n_in], *refs[n_in + n_after :])
        if placed:
            shard = lax.axis_index("shard")
            kernel((lax.axis_index("replica"), shard // 2, shard % 2), *refs)
        else:
            kernel(*refs)

    return pl.pallas_call(
        run,
        out_shape=out,
        in_specs=[SMEM if i < smem else HBM if i in hbm else VMEM for i in range(n_in)]
        + [ANY] * n_after,
        out_specs=HBM if out_hbm else [VMEM] * len(out) if many else VMEM,
        scratch_shapes=list(scratch),
        name=name,
        cost_estimate=pl.CostEstimate(flops=cost, bytes_accessed=0, transcendentals=0),
        compiler_params=pltpu.CompilerParams(vmem_limit_bytes=limit),
    )(*ins, *after)


def sds(shape, dtype=BF16):
    return jax.ShapeDtypeStruct(shape, dtype)


def aligned(index, size):
    return pl.ds(pl.multiple_of(index * size, size), size)


def start_all(pairs, sem):
    copies = [pltpu.make_async_copy(a, b, sem.at[i]) for i, (a, b) in enumerate(pairs)]
    for c in copies:
        c.start()
    return copies


def carry_kernel(me, weight, table, out, rows_in, part_in, sem):
    rows, cols = rows_in.shape
    part = part_in.shape[0]
    copies = start_all(
        [
            (table.at[:, aligned(me[0], cols)], rows_in),
            (weight.at[aligned(me[0], part), :], part_in),
        ],
        sem,
    )
    copies[1].wait()
    for i in range((out.shape[0] - cols) // part):
        out[cols + i * part : cols + (i + 1) * part, :] = part_in[:, i * rows : (i + 1) * rows]
    copies[0].wait()
    out[0:cols, :] = rows_in[...].T.astype(BF16)


def pack_kernel(lens, owner, local, q, k, out, ids, sem):
    n, rows, pw = out.shape
    tok = q.shape[0]
    runs = tok // pw
    later = start_all(
        [
            (x.at[:, i * pw : (i + 1) * pw], out.at[i, j * tok : (j + 1) * tok, :])
            for i in range(n)
            for j, x in enumerate((q, k))
        ],
        sem,
    )
    lane = iota((EXTRA, tok), 1)
    row = iota((EXTRA, tok), 0)
    seg = jnp.zeros((EXTRA, tok), F32)
    end = jnp.int32(0)
    for i in range(lens.shape[1]):
        end = end + lens[0, i]
        seg = seg + jnp.where(lane >= end, 1.0, 0.0)
    all_ids = jnp.where(
        row == 0,
        jnp.broadcast_to(owner[...].astype(F32), (EXTRA, tok)),
        jnp.where(
            row == 1,
            jnp.broadcast_to(local[...].astype(F32), (EXTRA, tok)),
            jnp.where(row == 2, seg, 0.0),
        ),
    ).astype(BF16)
    for i in range(runs):
        ids[i * EXTRA : (i + 1) * EXTRA, :] = all_ids[:, i * pw : (i + 1) * pw]
    later = later + start_all(
        [(ids, out.at[i, 2 * tok : rows, :]) for i in range(n)], sem.at[pl.ds(2 * n, n)]
    )
    for c in later:
        c.wait()


def pass_kernel(x, y, far_y, far_x, sem):
    half = far_x.shape[0]
    copies = start_all([(x.at[half:, :], far_y), (y.at[0:half, :], far_x)], sem)
    for c in copies:
        c.wait()


def stack_kernel(me, *refs):
    *blocks, out = refs
    cols = out.shape[1]
    for m, p in enumerate(blocks):
        out[me[1] ^ m] = p[0:cols, :]


def join_kernel(me, *refs):
    *parts, out = refs
    part = out.shape[0] // len(parts)
    rows = parts[0].shape[1]
    for m, p in enumerate(parts):
        for i in range(p.shape[0] // part):
            out[aligned(me[0] ^ m, part), i * rows : (i + 1) * rows] = p[i * part : (i + 1) * part, :]


def gate_kernel(out):
    out[...] = jnp.zeros_like(out)


def choose_kernel(me, *refs):
    n = (len(refs) - 1) // 2
    parts, out, held = refs[:n], refs[n : 2 * n], refs[2 * n]
    first = parts[0].shape[0] - held.shape[1]
    for m, p in enumerate(parts):
        held[m] = p[first:, :]
    for m, o in enumerate(out):
        o[...] = held[me[1] ^ me[0] ^ m]


def weights_kernel(me, packs, out):
    n, _, pw = packs.shape
    heads, tok = out.shape[1:3]
    dqk = pw // heads
    down, across = iota((tok, tok), 0), iota((tok, tok), 1)
    lane = iota((tok, pw), 1)
    for r in range(n):
        p = packs.at[me[0] ^ r]
        q = p[0:tok, :]
        k = p[tok : 2 * tok, :]
        seg = ids_of(packs, me[0] ^ r, tok)[2:3, :]
        seg_down = jnp.sum(jnp.where(down == across, seg, 0.0), axis=1, keepdims=True)
        mask = (seg == seg_down) & (down <= across)
        for j in range(heads):
            kj = jnp.where(lane // dqk == j, k, jnp.zeros_like(k))
            s = nt(kj, q) * dqk ** (-0.5)
            w = s / (1.0 + jnp.exp(-s)) * (1.0 / MAXLEN)
            out[r, j] = jnp.where(mask, w, 0.0).astype(BF16)


def ids_of(packs, r, tok):
    runs = tok // packs.shape[2]
    ids = packs[r, 2 * tok : 2 * tok + runs * EXTRA, :].astype(F32)
    return jnp.concatenate([ids[i * EXTRA : (i + 1) * EXTRA] for i in range(runs)], axis=1)


def one_hot(ids, shard, rows):
    own, loc = ids[0:1, :], ids[1:2, :]
    named = jnp.where(own == shard.astype(F32), loc, -1.0)
    at = iota((rows, ids.shape[1]), 0).astype(F32)
    return jnp.where(at == named, 1.0, 0.0).astype(BF16)


def mix_kernel(me, packs, w, mine, other, out):
    n, cols, rows = mine.shape
    heads, tok = w.shape[1:3]
    dv = cols // heads
    blocks = jnp.concatenate([x[z] for z in range(n) for x in (mine, other)], axis=1)
    for r in range(n):
        ids = ids_of(packs, me[0] ^ r, w.shape[2])
        picks = jnp.concatenate(
            [one_hot(ids, 2 * z + (me[2] ^ cc), rows) for z in range(n) for cc in range(2)], axis=0
        )
        vals = nn(blocks, picks).astype(BF16)
        for j in range(heads):
            out[j * dv : (j + 1) * dv, r * tok : (r + 1) * tok] = nn(
                vals[j * dv : (j + 1) * dv, :], w[r, j]
            ).astype(BF16)


def by_row(me, packs, grad, core, z, rows):
    n = packs.shape[0]
    tok = grad.shape[0] // n
    ids = jnp.concatenate([ids_of(packs, me[0] ^ r, tok) for r in range(n)], axis=1)
    return nn(one_hot(ids, 2 * z + core, rows), grad[...])


def back_kernel(me, packs, ow_mine, ow_other, w, *refs):
    *cots, send, grad, ow = refs
    n = packs.shape[0]
    heads, tok = w.shape[1:3]
    head_rows = ow_mine.shape[0]
    ow[aligned(me[2], head_rows), :] = ow_mine[...]
    ow[aligned(1 - me[2], head_rows), :] = ow_other[...]
    first = 0
    for cot in cots:
        end = first + cot.shape[0]
        grad[first:end, :] = nt(cot[...], ow[...]).astype(BF16)
        first = end
    for r in range(n):
        at_r = slice(r * tok, (r + 1) * tok)
        for j in range(heads):
            at_j = slice(j * head_rows, (j + 1) * head_rows)
            grad[at_r, at_j] = nn(w[r, j], grad[at_r, at_j]).astype(BF16)
    for z in range(n):
        send[z] = by_row(me, packs, grad, 1 - me[2], z, send.shape[1]).astype(BF16)


def keep_kernel(me, packs, grad, keep):
    for z in range(keep.shape[0]):
        keep[z] = by_row(me, packs, grad, me[2], z, keep.shape[1])


def wgrad_kernel(me, mixed, *refs):
    *cots, keep, send = refs
    rows = keep.shape[0]
    for cc, out in ((1, send), (0, keep)):
        at = aligned(me[2] ^ cc, rows)
        total = jnp.zeros(keep.shape, F32)
        first = 0
        for cot in cots:
            end = first + cot.shape[0]
            total = total + nn(mixed[at, first:end], cot[...])
            first = end
        out[...] = total.astype(out.dtype)


def add_kernel(keep, got, out):
    out[...] = (keep[...] + got[...].astype(F32)).astype(out.dtype)


def add_parts_kernel(me, keep, got, *out):
    rows = out[0].shape[0]
    for m, o in enumerate(out):
        at = aligned(me[0] ^ m, rows)
        o[...] = (keep[at, :] + got[at, :].astype(F32)).astype(o.dtype)


def sum_first_kernel(parts, out):
    total = parts[0].astype(F32)
    for m in range(1, parts.shape[0]):
        total = total + parts[m].astype(F32)
    out[...] = total.astype(out.dtype)


def sum_kernel(*refs):
    *parts, out = refs
    total = parts[0][...].astype(F32)
    for p in parts[1:]:
        total = total + p[...].astype(F32)
    out[...] = total.astype(out.dtype)


def place_kernel(me, *refs):
    *parts, out = refs
    rows = parts[0].shape[0]
    for m, p in enumerate(parts):
        out[aligned(me[0] ^ m, rows), :] = p[...]


def update_kernel(me, table, accum, *refs):
    *parts, new_table, new_accum, grad = refs
    rows, width = table.shape
    cols = width // len(parts)
    for m, p in enumerate(parts):
        grad[:, aligned(me[0] ^ m, cols)] = p[...].astype(F32)
    mean = jnp.sum(grad[...] * grad[...], axis=1, keepdims=True) * (1.0 / width)
    same = iota((rows, rows), 0) == iota((rows, rows), 1)
    old = jnp.sum(jnp.where(same, accum[...], 0.0), axis=1, keepdims=True)
    fresh = old + mean
    new_accum[...] = jnp.sum(jnp.where(same, fresh, 0.0), axis=0, keepdims=True)
    new_table[...] = table[...] - grad[...] / (jnp.sqrt(fresh) + 1e-08)


def body(table, accum, owner, local_row, lengths, queries, keys, cotangent, out_weight):
    n = lax.axis_size("replica")
    shards = lax.axis_size("shard")
    tok = owner.shape[0]
    rows, width = table.shape
    cols = width // n
    heads = HEADS // n
    part = out_weight.shape[0] // n

    def column(x, m):
        return lax.ppermute(x, "replica", [(i, i ^ m) for i in range(n)]) if m else x

    def along(x, m):
        return lax.ppermute(x, "shard", [(i, i ^ (2 * m)) for i in range(shards)]) if m else x

    def core(x):
        return lax.ppermute(x, "shard", [(i, i ^ 1) for i in range(shards)])

    def swap_along(x):
        groups = [list(range(c, shards, 2)) for c in range(2)]
        return lax.all_to_all(x, "shard", 0, 0, tiled=True, axis_index_groups=groups)

    def swap_columns(x):
        return lax.all_to_all(x, "replica", 0, 0, tiled=True)

    half = tok // 2
    x, y = column(cotangent, 1), column(cotangent, 2)
    zrows = cols + part * width // rows
    zpay = call(
        carry_kernel,
        "carry",
        sds((zrows, rows)),
        (out_weight, table),
        hbm=(0, 1),
        scratch=[
            pltpu.VMEM((rows, cols), F32),
            pltpu.VMEM((part, width), BF16),
            pltpu.SemaphoreType.DMA((2,)),
        ],
        limit=None,
        placed=True,
    )
    pw = queries.shape[1] // n
    packs = call(
        pack_kernel,
        "pack",
        sds((n, 2 * tok + tok // pw * EXTRA, pw)),
        (lengths, owner.reshape(1, tok), local_row.reshape(1, tok), queries, keys),
        smem=1,
        out_hbm=True,
        scratch=[
            pltpu.VMEM((tok // pw * EXTRA, pw), BF16),
            pltpu.SemaphoreType.DMA((3 * n,)),
        ],
    )
    packs = swap_columns(packs)
    blocks = [along(zpay, m) for m in range(n)]
    far_y, far_x = call(
        pass_kernel,
        "pass",
        [sds((half, width))] * 2,
        (x, y),
        scratch=[pltpu.SemaphoreType.DMA((2,))],
        cost=PASS_COST,
    )
    w = call(
        weights_kernel,
        "weights",
        sds((n, heads, tok, tok)),
        (packs,),
        after=(far_x,),
        placed=True,
    )
    owp = call(
        choose_kernel,
        "choose",
        [sds((zrows - cols, rows))] * n,
        blocks,
        after=(packs,),
        scratch=[pltpu.VMEM((n, zrows - cols, rows), BF16)],
        placed=True,
    )
    mine = call(
        stack_kernel, "stack", sds((n, cols, rows)), blocks, after=(owp[0],), placed=True
    )
    other = core(mine)
    owp = [column(p, m) for m, p in enumerate(owp)]
    ow_mine = call(join_kernel, "join", sds((n * part, width)), owp, placed=True)
    ow_other = core(ow_mine)
    far_y, far_x = column(far_y, 2), column(far_x, 1)
    cots = [cotangent, x, y, far_x, far_y]
    here = call(gate_kernel, "gate", sds((8, 128), F32), (), after=(far_x, far_y), cost=GATE_COST)

    mixed = call(
        mix_kernel, "mix", sds((cols, n * tok)), (packs, w, mine, other), placed=True
    )
    send, grad = call(
        back_kernel,
        "back",
        [sds((n, rows, cols)), sds((n * tok, cols))],
        (packs, ow_mine, ow_other, w, *cots),
        after=(here, mixed),
        scratch=[pltpu.VMEM((cols, width), BF16)],
        placed=True,
    )
    got = core(send)
    keep = call(keep_kernel, "keep", sds((n, rows, cols), F32), (packs, grad), placed=True)
    sums = call(add_kernel, "add", sds((n, rows, cols)), (keep, got))
    ready = sums
    sums = swap_along(sums)
    wkeep, wsend = call(
        wgrad_kernel,
        "wgrad",
        [sds((n * part, width), F32), sds((n * part, width))],
        (mixed, *cots),
        after=(ready,),
        placed=True,
    )
    wgot = core(wsend)

    wparts = call(
        add_parts_kernel, "add_parts", [sds((part, width))] * n, (wkeep, wgot), placed=True
    )
    wparts = [column(p, m) for m, p in enumerate(wparts)]
    wparts = call(
        choose_kernel,
        "pick",
        [sds((part, width))] * n,
        wparts,
        placed=True,
        scratch=[pltpu.VMEM((n, part, width), BF16)],
    )
    wparts = [along(p, m) for m, p in enumerate(wparts)]

    grad = call(sum_first_kernel, "sum_rows", sds((rows, cols)), (sums,))
    grads = [column(grad, m) for m in range(n)]
    there = call(
        gate_kernel,
        "gate_parts",
        sds((8, 128), F32),
        (),
        after=tuple(wparts[1:]),
        cost=PARTS_COST,
    )
    wsum = call(sum_kernel, "sum_parts", sds((part, width)), wparts, after=(grad, there))
    wsums = [column(wsum, m) for m in range(n)]
    new_table, new_accum = call(
        update_kernel,
        "update",
        [sds((rows, width), F32), sds((1, rows), F32)],
        (table, accum.reshape(1, rows), *grads),
        cost=UPDATE_COST,
        placed=True,
        scratch=[pltpu.VMEM((rows, width), F32)],
    )
    weight_grad = call(
        place_kernel, "place", sds((n * part, width)), wsums, after=(new_accum,), placed=True
    )
    return (new_table, new_accum.reshape(rows), weight_grad)


def fits(mesh):
    n, shards = mesh.shape["replica"], mesh.shape["shard"]
    return n & (n - 1) == 0 and shards == HEADS and 2 * n == HEADS


def solution(mesh):
    placed = (
        P("shard", None),
        P("shard"),
        P(("replica", "shard"), None),
        P(("replica", "shard")),
        P(("replica", "shard"), None),
        P(("replica", "shard"), None),
        P(("replica", "shard"), None),
        P(("replica", "shard"), None),
        P("shard", None),
    )
    return jax.shard_map(
        body if fits(mesh) else general_body,
        mesh=mesh,
        in_specs=placed,
        out_specs=(P("shard", None), P("shard"), P("shard", None)),
        check_vma=False,
    )
```

```python
import functools

import jax
import jax.numpy as jnp
from jax import lax
from jax.experimental import pallas as pl
from jax.experimental.pallas import tpu as pltpu
from jax.sharding import PartitionSpec as P

HEADS = 8
MAXLEN = 128
PASS_COST = 12 * 10**9
PARTS_COST = 4 * 10**9
UPDATE_COST = 8 * 10**9
GATE_COST = 8 * 10**9
EXTRA = 16
VMEM = pl.BlockSpec(memory_space=pltpu.VMEM)
ANY = pl.BlockSpec(memory_space=pl.ANY)
HBM = pl.BlockSpec(memory_space=pltpu.HBM)
SMEM = pl.BlockSpec(memory_space=pltpu.SMEM)
F32 = jnp.float32
BF16 = jnp.bfloat16


def adagrad(table_rows, accum_rows, grad_rows):
    new_accum = accum_rows + jnp.mean(grad_rows * grad_rows, axis=1)
    new_table = table_rows - 1.0 * grad_rows / (jnp.sqrt(new_accum)[:, None] + 1e-08)
    return (new_table, new_accum)


def general_body(
    table, accum, owner, local_row, lengths, queries, keys, cotangent, out_weight
):
    shards = lax.axis_size("shard")
    tok = owner.shape[0]
    rows_dev = table.shape[0]
    width = table.shape[1]
    heads = HEADS
    dqk = queries.shape[1] // heads
    dval = width // heads
    slots = 2 * tok // shards
    dest = owner[:, 0]
    onehot = (dest[:, None] == jnp.arange(shards)[None, :]).astype(jnp.bfloat16)
    pos = jnp.arange(tok)
    lower = (pos[None, :] < pos[:, None]).astype(jnp.bfloat16)
    before = jnp.dot(lower, onehot, preferred_element_type=jnp.float32)
    rank = jnp.sum(before * onehot.astype(jnp.float32), axis=1).astype(jnp.int32)
    slot = dest * slots + rank
    send_idx = (
        jnp.full((shards * slots,), -1, jnp.int32).at[slot].set(local_row).reshape(shards, slots)
    )
    recv_idx = lax.all_to_all(send_idx, "shard", split_axis=0, concat_axis=0, tiled=True).reshape(
        -1
    )
    valid = recv_idx >= 0
    picked = jnp.take(table, jnp.clip(recv_idx, 0, rows_dev - 1), axis=0)
    picked = (
        jnp.where(valid[:, None], picked, 0.0).astype(jnp.bfloat16).reshape(shards, slots, width)
    )
    ends = jnp.cumsum(lengths[0])
    seg = jnp.sum((pos[:, None] >= ends[None, :]).astype(jnp.int32), axis=1)
    mask = ((seg[:, None] == seg[None, :]) & (pos[None, :] <= pos[:, None])).astype(jnp.float32)
    q3 = queries.reshape(tok, heads, dqk)
    k3 = keys.reshape(tok, heads, dqk)
    scores = jnp.einsum("ihd,jhd->hij", q3, k3, preferred_element_type=jnp.float32) * dqk ** (-0.5)
    weights = (jax.nn.silu(scores) / MAXLEN * mask[None]).astype(jnp.bfloat16)
    fetched = lax.all_to_all(picked, "shard", split_axis=0, concat_axis=0, tiled=True).reshape(
        shards * slots, width
    )
    embedded = fetched[slot]
    vals = embedded.reshape(tok, heads, dval)
    mixed = (
        jnp.einsum("hij,jhd->ihd", weights, vals, preferred_element_type=jnp.float32)
        .reshape(tok, width)
        .astype(jnp.bfloat16)
    )
    back = lax.dot_general(
        cotangent,
        lax.all_gather(out_weight, "shard", axis=0, tiled=True),
        (((1,), (1,)), ((), ())),
        preferred_element_type=jnp.float32,
    ).astype(jnp.bfloat16)
    grad_share = lax.psum_scatter(
        lax.dot_general(
            mixed, cotangent, (((0,), (0,)), ((), ())), preferred_element_type=jnp.float32
        ),
        "shard",
        scatter_dimension=0,
        tiled=True,
    )
    weight_grad = lax.psum(grad_share, "replica").astype(jnp.bfloat16)
    b3 = back.reshape(tok, heads, dval)
    token_grad = jnp.einsum(
        "hij,ihd->jhd", weights, b3, preferred_element_type=jnp.float32
    ).reshape(tok, width)
    send_grad = (
        jnp.zeros((shards * slots, width), jnp.float32)
        .at[slot]
        .set(token_grad)
        .reshape(shards, slots, width)
    )
    arrived = (
        lax.all_to_all(
            send_grad.astype(jnp.bfloat16), "shard", split_axis=0, concat_axis=0, tiled=True
        )
        .astype(send_grad.dtype)
        .reshape(shards * slots, width)
    )
    select = (recv_idx[:, None] == jnp.arange(rows_dev)[None, :]).astype(jnp.float32)
    grad_rows = lax.dot_general(
        select,
        arrived,
        (((0,), (0,)), ((), ())),
        precision=lax.Precision.HIGHEST,
        preferred_element_type=jnp.float32,
    )
    share = lax.psum_scatter(
        grad_rows.astype(jnp.bfloat16), "replica", scatter_dimension=0, tiled=True
    ).astype(jnp.float32)
    quarter = share.shape[0]
    first = lax.axis_index("replica") * quarter
    part_table = lax.dynamic_slice_in_dim(table, first, quarter, 0)
    part_accum = lax.dynamic_slice_in_dim(accum, first, quarter, 0)
    upd_table, upd_accum = adagrad(part_table, part_accum, share)
    new_table, new_accum = (
        lax.all_gather(upd_table, "replica", axis=0, tiled=True),
        lax.all_gather(upd_accum, "replica", axis=0, tiled=True),
    )
    return (new_table, new_accum, weight_grad)


def iota(shape, axis):
    return lax.broadcasted_iota(jnp.int32, shape, axis)


def nt(a, b):
    return lax.dot_general(a, b, (((1,), (1,)), ((), ())), preferred_element_type=F32)


def nn(a, b):
    return lax.dot_general(a, b, (((1,), (0,)), ((), ())), preferred_element_type=F32)


def call(
    kernel,
    name,
    out,
    ins,
    smem=0,
    after=(),
    scratch=(),
    hbm=(),
    limit=16 << 20,
    cost=0,
    placed=False,
    out_hbm=False,
):
    n_in, n_after = len(ins), len(after)
    many = isinstance(out, (list, tuple))

    def run(*refs):
        refs = (*refs[:n_in], *refs[n_in + n_after :])
        if placed:
            shard = lax.axis_index("shard")
            kernel((lax.axis_index("replica"), shard // 2, shard % 2), *refs)
        else:
            kernel(*refs)

    return pl.pallas_call(
        run,
        out_shape=out,
        in_specs=[SMEM if i < smem else HBM if i in hbm else VMEM for i in range(n_in)]
        + [ANY] * n_after,
        out_specs=HBM if out_hbm else [VMEM] * len(out) if many else VMEM,
        scratch_shapes=list(scratch),
        name=name,
        cost_estimate=pl.CostEstimate(flops=cost, bytes_accessed=0, transcendentals=0),
        compiler_params=pltpu.CompilerParams(vmem_limit_bytes=limit),
    )(*ins, *after)


def sds(shape, dtype=BF16):
    return jax.ShapeDtypeStruct(shape, dtype)


def aligned(index, size):
    return pl.ds(pl.multiple_of(index * size, size), size)


def start_all(pairs, sem):
    copies = [pltpu.make_async_copy(a, b, sem.at[i]) for i, (a, b) in enumerate(pairs)]
    for c in copies:
        c.start()
    return copies


def carry_kernel(me, weight, table, out, rows_in, part_in, sem):
    rows, cols = rows_in.shape
    part = part_in.shape[0]
    copies = start_all(
        [
            (table.at[:, aligned(me[0], cols)], rows_in),
            (weight.at[aligned(me[0], part), :], part_in),
        ],
        sem,
    )
    copies[1].wait()
    for i in range((out.shape[0] - rows) // part):
        out[rows + i * part : rows + (i + 1) * part, :] = part_in[:, i * cols : (i + 1) * cols]
    copies[0].wait()
    out[0:rows, :] = rows_in[...].astype(BF16)


def pack_kernel(lens, owner, local, q, k, out, ids, sem):
    n, rows, pw = out.shape
    tok = q.shape[0]
    runs = tok // pw
    later = start_all(
        [
            (x.at[:, i * pw : (i + 1) * pw], out.at[i, j * tok : (j + 1) * tok, :])
            for i in range(n)
            for j, x in enumerate((q, k))
        ],
        sem,
    )
    lane = iota((EXTRA, tok), 1)
    row = iota((EXTRA, tok), 0)
    seg = jnp.zeros((EXTRA, tok), F32)
    end = jnp.int32(0)
    for i in range(lens.shape[1]):
        end = end + lens[0, i]
        seg = seg + jnp.where(lane >= end, 1.0, 0.0)
    all_ids = jnp.where(
        row == 0,
        jnp.broadcast_to(owner[...].astype(F32), (EXTRA, tok)),
        jnp.where(
            row == 1,
            jnp.broadcast_to(local[...].astype(F32), (EXTRA, tok)),
            jnp.where(row == 2, seg, 0.0),
        ),
    ).astype(BF16)
    for i in range(runs):
        ids[i * EXTRA : (i + 1) * EXTRA, :] = all_ids[:, i * pw : (i + 1) * pw]
    later = later + start_all(
        [(ids, out.at[i, 2 * tok : rows, :]) for i in range(n)], sem.at[pl.ds(2 * n, n)]
    )
    for c in later:
        c.wait()


def pass_kernel(x, y, far_y, far_x, sem):
    half = far_x.shape[0]
    copies = start_all([(x.at[half:, :], far_y), (y.at[0:half, :], far_x)], sem)
    for c in copies:
        c.wait()


def stack_kernel(me, *refs):
    *blocks, out = refs
    rows = out.shape[1]
    for m, p in enumerate(blocks):
        out[me[1] ^ m] = p[0:rows, :]


def join_kernel(me, *refs):
    *parts, out = refs
    part = out.shape[0] // len(parts)
    rows = parts[0].shape[1]
    for m, p in enumerate(parts):
        for i in range(p.shape[0] // part):
            out[aligned(me[0] ^ m, part), i * rows : (i + 1) * rows] = p[i * part : (i + 1) * part, :]


def gate_kernel(out):
    out[...] = jnp.zeros_like(out)


def choose_kernel(me, *refs):
    n = (len(refs) - 1) // 2
    parts, out, held = refs[:n], refs[n : 2 * n], refs[2 * n]
    first = parts[0].shape[0] - held.shape[1]
    for m, p in enumerate(parts):
        held[m] = p[first:, :]
    for m, o in enumerate(out):
        o[...] = held[me[1] ^ me[0] ^ m]


def weights_kernel(me, packs, out):
    n, _, pw = packs.shape
    heads, tok = out.shape[1:3]
    dqk = pw // heads
    down, across = iota((tok, tok), 0), iota((tok, tok), 1)
    lane = iota((tok, pw), 1)
    for r in range(n):
        p = packs.at[me[0] ^ r]
        q = p[0:tok, :]
        k = p[tok : 2 * tok, :]
        seg = ids_of(packs, me[0] ^ r, tok)[2:3, :]
        seg_down = jnp.sum(jnp.where(down == across, seg, 0.0), axis=1, keepdims=True)
        mask = (seg == seg_down) & (down <= across)
        for j in range(heads):
            kj = jnp.where(lane // dqk == j, k, jnp.zeros_like(k))
            s = nt(kj, q) * dqk ** (-0.5)
            w = s / (1.0 + jnp.exp(-s)) * (1.0 / MAXLEN)
            out[r, j] = jnp.where(mask, w, 0.0).astype(BF16)


def ids_of(packs, r, tok):
    runs = tok // packs.shape[2]
    ids = packs[r, 2 * tok : 2 * tok + runs * EXTRA, :].astype(F32)
    return jnp.concatenate([ids[i * EXTRA : (i + 1) * EXTRA] for i in range(runs)], axis=1)


def one_hot(ids, shard, rows):
    own, loc = ids[0:1, :], ids[1:2, :]
    named = jnp.where(own == shard.astype(F32), loc, -1.0)
    at = iota((rows, ids.shape[1]), 0).astype(F32)
    return jnp.where(at == named, 1.0, 0.0).astype(BF16)


def mix_kernel(me, packs, w, mine, other, out, picks):
    n, rows, cols = mine.shape
    heads, tok = w.shape[1:3]
    dv = cols // heads
    same = iota((tok, tok), 0) == iota((tok, tok), 1)
    at = iota((tok, rows), 1).astype(F32)
    for r in range(n):
        ids = ids_of(packs, me[0] ^ r, tok)
        own = jnp.sum(jnp.where(same, ids[0:1, :], 0.0), axis=1, keepdims=True)
        loc = jnp.sum(jnp.where(same, ids[1:2, :], 0.0), axis=1, keepdims=True)
        for z in range(n):
            for cc in range(2):
                shard = (2 * z + (me[2] ^ cc)).astype(F32)
                named = jnp.where(own == shard, loc, -1.0)
                first = (2 * z + cc) * rows
                picks[r * tok : (r + 1) * tok, first : first + rows] = jnp.where(
                    at == named, 1.0, 0.0
                ).astype(BF16)
    blocks = jnp.concatenate([x[z] for z in range(n) for x in (mine, other)], axis=0)
    vals = nn(picks[...], blocks).astype(BF16)
    for r in range(n):
        turned = vals[r * tok : (r + 1) * tok, :].T
        for j in range(heads):
            out[j * dv : (j + 1) * dv, r * tok : (r + 1) * tok] = nn(
                turned[j * dv : (j + 1) * dv, :], w[r, j]
            ).astype(BF16)


def by_row(me, packs, grad, core, out):
    n, rows, _ = out.shape
    tok = grad.shape[0] // n
    ids = jnp.concatenate([ids_of(packs, me[0] ^ r, tok) for r in range(n)], axis=1)
    picks = jnp.concatenate([one_hot(ids, 2 * z + core, rows) for z in range(n)], axis=0)
    total = nn(picks, grad[...])
    for z in range(n):
        out[z] = total[z * rows : (z + 1) * rows, :].astype(out.dtype)


def back_kernel(me, packs, ow_mine, ow_other, w, *refs):
    *cots, send, grad, ow = refs
    n = packs.shape[0]
    heads, tok = w.shape[1:3]
    head_rows = ow_mine.shape[0]
    ow[aligned(me[2], head_rows), :] = ow_mine[...]
    ow[aligned(1 - me[2], head_rows), :] = ow_other[...]
    first = 0
    for cot in cots:
        end = first + cot.shape[0]
        grad[first:end, :] = nt(cot[...], ow[...]).astype(BF16)
        first = end
    for r in range(n):
        at_r = slice(r * tok, (r + 1) * tok)
        for j in range(heads):
            at_j = slice(j * head_rows, (j + 1) * head_rows)
            grad[at_r, at_j] = nn(w[r, j], grad[at_r, at_j]).astype(BF16)
    by_row(me, packs, grad, 1 - me[2], send)


def keep_kernel(me, packs, grad, keep):
    by_row(me, packs, grad, me[2], keep)


def wgrad_kernel(me, mixed, *refs):
    *cots, keep, send = refs
    rows = keep.shape[0]
    for cc, out in ((1, send), (0, keep)):
        at = aligned(me[2] ^ cc, rows)
        total = jnp.zeros(keep.shape, F32)
        first = 0
        for cot in cots:
            end = first + cot.shape[0]
            total = total + nn(mixed[at, first:end], cot[...])
            first = end
        out[...] = total.astype(out.dtype)


def add_kernel(keep, got, out):
    out[...] = (keep[...] + got[...].astype(F32)).astype(out.dtype)


def add_parts_kernel(me, keep, got, *out):
    rows = out[0].shape[0]
    for m, o in enumerate(out):
        at = aligned(me[0] ^ m, rows)
        o[...] = (keep[at, :] + got[at, :].astype(F32)).astype(o.dtype)


def sum_first_kernel(parts, out):
    total = parts[0].astype(F32)
    for m in range(1, parts.shape[0]):
        total = total + parts[m].astype(F32)
    out[...] = total.astype(out.dtype)


def sum_kernel(*refs):
    *parts, out = refs
    total = parts[0][...].astype(F32)
    for p in parts[1:]:
        total = total + p[...].astype(F32)
    out[...] = total.astype(out.dtype)


def place_kernel(me, *refs):
    *parts, out = refs
    rows = parts[0].shape[0]
    for m, p in enumerate(parts):
        out[aligned(me[0] ^ m, rows), :] = p[...]


def update_kernel(me, table, accum, *refs):
    *parts, new_table, new_accum, grad = refs
    rows, width = table.shape
    cols = width // len(parts)
    for m, p in enumerate(parts):
        grad[:, aligned(me[0] ^ m, cols)] = p[...].astype(F32)
    mean = jnp.sum(grad[...] * grad[...], axis=1, keepdims=True) * (1.0 / width)
    same = iota((rows, rows), 0) == iota((rows, rows), 1)
    old = jnp.sum(jnp.where(same, accum[...], 0.0), axis=1, keepdims=True)
    fresh = old + mean
    new_accum[...] = jnp.sum(jnp.where(same, fresh, 0.0), axis=0, keepdims=True)
    new_table[...] = table[...] - grad[...] / (jnp.sqrt(fresh) + 1e-08)


def body(table, accum, owner, local_row, lengths, queries, keys, cotangent, out_weight):
    n = lax.axis_size("replica")
    shards = lax.axis_size("shard")
    tok = owner.shape[0]
    rows, width = table.shape
    cols = width // n
    heads = HEADS // n
    part = out_weight.shape[0] // n

    def column(x, m):
        return lax.ppermute(x, "replica", [(i, i ^ m) for i in range(n)]) if m else x

    def along(x, m):
        return lax.ppermute(x, "shard", [(i, i ^ (2 * m)) for i in range(shards)]) if m else x

    def core(x):
        return lax.ppermute(x, "shard", [(i, i ^ 1) for i in range(shards)])

    def swap_along(x):
        groups = [list(range(c, shards, 2)) for c in range(2)]
        return lax.all_to_all(x, "shard", 0, 0, tiled=True, axis_index_groups=groups)

    def swap_columns(x):
        return lax.all_to_all(x, "replica", 0, 0, tiled=True)

    half = tok // 2
    x, y = column(cotangent, 1), column(cotangent, 2)
    zrows = rows + part * width // cols
    zpay = call(
        carry_kernel,
        "carry",
        sds((zrows, cols)),
        (out_weight, table),
        hbm=(0, 1),
        scratch=[
            pltpu.VMEM((rows, cols), F32),
            pltpu.VMEM((part, width), BF16),
            pltpu.SemaphoreType.DMA((2,)),
        ],
        limit=None,
        placed=True,
    )
    pw = queries.shape[1] // n
    packs = call(
        pack_kernel,
        "pack",
        sds((n, 2 * tok + tok // pw * EXTRA, pw)),
        (lengths, owner.reshape(1, tok), local_row.reshape(1, tok), queries, keys),
        smem=1,
        out_hbm=True,
        scratch=[
            pltpu.VMEM((tok // pw * EXTRA, pw), BF16),
            pltpu.SemaphoreType.DMA((3 * n,)),
        ],
    )
    packs = swap_columns(packs)
    blocks = [along(zpay, m) for m in range(n)]
    far_y, far_x = call(
        pass_kernel,
        "pass",
        [sds((half, width))] * 2,
        (x, y),
        scratch=[pltpu.SemaphoreType.DMA((2,))],
        cost=PASS_COST,
    )
    w = call(
        weights_kernel,
        "weights",
        sds((n, heads, tok, tok)),
        (packs,),
        after=(far_x,),
        placed=True,
    )
    owp = call(
        choose_kernel,
        "choose",
        [sds((zrows - rows, cols))] * n,
        blocks,
        after=(packs,),
        scratch=[pltpu.VMEM((n, zrows - rows, cols), BF16)],
        placed=True,
    )
    mine = call(
        stack_kernel, "stack", sds((n, rows, cols)), blocks, after=(owp[0],), placed=True
    )
    other = core(mine)
    owp = [column(p, m) for m, p in enumerate(owp)]
    ow_mine = call(join_kernel, "join", sds((n * part, width)), owp, placed=True)
    ow_other = core(ow_mine)
    far_y, far_x = column(far_y, 2), column(far_x, 1)
    cots = [cotangent, x, y, far_x, far_y]
    here = call(gate_kernel, "gate", sds((8, 128), F32), (), after=(far_x, far_y), cost=GATE_COST)

    mixed = call(
        mix_kernel,
        "mix",
        sds((cols, n * tok)),
        (packs, w, mine, other),
        scratch=[pltpu.VMEM((n * tok, shards * rows), BF16)],
        placed=True,
    )
    send, grad = call(
        back_kernel,
        "back",
        [sds((n, rows, cols)), sds((n * tok, cols))],
        (packs, ow_mine, ow_other, w, *cots),
        after=(here, mixed),
        scratch=[pltpu.VMEM((cols, width), BF16)],
        placed=True,
    )
    got = core(send)
    keep = call(keep_kernel, "keep", sds((n, rows, cols), F32), (packs, grad), placed=True)
    sums = call(add_kernel, "add", sds((n, rows, cols)), (keep, got))
    ready = sums
    sums = swap_along(sums)
    wkeep, wsend = call(
        wgrad_kernel,
        "wgrad",
        [sds((n * part, width), F32), sds((n * part, width))],
        (mixed, *cots),
        after=(ready,),
        placed=True,
    )
    wgot = core(wsend)

    wparts = call(
        add_parts_kernel, "add_parts", [sds((part, width))] * n, (wkeep, wgot), placed=True
    )
    wparts = [column(p, m) for m, p in enumerate(wparts)]
    wparts = call(
        choose_kernel,
        "pick",
        [sds((part, width))] * n,
        wparts,
        placed=True,
        scratch=[pltpu.VMEM((n, part, width), BF16)],
    )
    wparts = [along(p, m) for m, p in enumerate(wparts)]

    grad = call(sum_first_kernel, "sum_rows", sds((rows, cols)), (sums,))
    grads = [column(grad, m) for m in range(n)]
    there = call(
        gate_kernel,
        "gate_parts",
        sds((8, 128), F32),
        (),
        after=tuple(wparts[1:]),
        cost=PARTS_COST,
    )
    wsum = call(sum_kernel, "sum_parts", sds((part, width)), wparts, after=(grad, there))
    wsums = [column(wsum, m) for m in range(n)]
    new_table, new_accum = call(
        update_kernel,
        "update",
        [sds((rows, width), F32), sds((1, rows), F32)],
        (table, accum.reshape(1, rows), *grads),
        cost=UPDATE_COST,
        placed=True,
        scratch=[pltpu.VMEM((rows, width), F32)],
    )
    weight_grad = call(
        place_kernel, "place", sds((n * part, width)), wsums, after=(new_accum,), placed=True
    )
    return (new_table, new_accum.reshape(rows), weight_grad)


def fits(mesh):
    n, shards = mesh.shape["replica"], mesh.shape["shard"]
    return n & (n - 1) == 0 and shards == HEADS and 2 * n == HEADS


def solution(mesh):
    placed = (
        P("shard", None),
        P("shard"),
        P(("replica", "shard"), None),
        P(("replica", "shard")),
        P(("replica", "shard"), None),
        P(("replica", "shard"), None),
        P(("replica", "shard"), None),
        P(("replica", "shard"), None),
        P("shard", None),
    )
    return jax.shard_map(
        body if fits(mesh) else general_body,
        mesh=mesh,
        in_specs=placed,
        out_specs=(P("shard", None), P("shard"), P("shard", None)),
        check_vma=False,
    )
```

```python
import functools

import jax
import jax.numpy as jnp
from jax import lax
from jax.experimental import pallas as pl
from jax.experimental.pallas import tpu as pltpu
from jax.sharding import PartitionSpec as P

HEADS = 8
MAXLEN = 128
PASS_COST = 12 * 10**9
PARTS_COST = 4 * 10**9
UPDATE_COST = 8 * 10**9
GATE_COST = 8 * 10**9
EXTRA = 16
VMEM = pl.BlockSpec(memory_space=pltpu.VMEM)
ANY = pl.BlockSpec(memory_space=pl.ANY)
HBM = pl.BlockSpec(memory_space=pltpu.HBM)
SMEM = pl.BlockSpec(memory_space=pltpu.SMEM)
F32 = jnp.float32
BF16 = jnp.bfloat16


def adagrad(table_rows, accum_rows, grad_rows):
    new_accum = accum_rows + jnp.mean(grad_rows * grad_rows, axis=1)
    new_table = table_rows - 1.0 * grad_rows / (jnp.sqrt(new_accum)[:, None] + 1e-08)
    return (new_table, new_accum)


def general_body(
    table, accum, owner, local_row, lengths, queries, keys, cotangent, out_weight
):
    shards = lax.axis_size("shard")
    tok = owner.shape[0]
    rows_dev = table.shape[0]
    width = table.shape[1]
    heads = HEADS
    dqk = queries.shape[1] // heads
    dval = width // heads
    slots = 2 * tok // shards
    dest = owner[:, 0]
    onehot = (dest[:, None] == jnp.arange(shards)[None, :]).astype(jnp.bfloat16)
    pos = jnp.arange(tok)
    lower = (pos[None, :] < pos[:, None]).astype(jnp.bfloat16)
    before = jnp.dot(lower, onehot, preferred_element_type=jnp.float32)
    rank = jnp.sum(before * onehot.astype(jnp.float32), axis=1).astype(jnp.int32)
    slot = dest * slots + rank
    send_idx = (
        jnp.full((shards * slots,), -1, jnp.int32).at[slot].set(local_row).reshape(shards, slots)
    )
    recv_idx = lax.all_to_all(send_idx, "shard", split_axis=0, concat_axis=0, tiled=True).reshape(
        -1
    )
    valid = recv_idx >= 0
    picked = jnp.take(table, jnp.clip(recv_idx, 0, rows_dev - 1), axis=0)
    picked = (
        jnp.where(valid[:, None], picked, 0.0).astype(jnp.bfloat16).reshape(shards, slots, width)
    )
    ends = jnp.cumsum(lengths[0])
    seg = jnp.sum((pos[:, None] >= ends[None, :]).astype(jnp.int32), axis=1)
    mask = ((seg[:, None] == seg[None, :]) & (pos[None, :] <= pos[:, None])).astype(jnp.float32)
    q3 = queries.reshape(tok, heads, dqk)
    k3 = keys.reshape(tok, heads, dqk)
    scores = jnp.einsum("ihd,jhd->hij", q3, k3, preferred_element_type=jnp.float32) * dqk ** (-0.5)
    weights = (jax.nn.silu(scores) / MAXLEN * mask[None]).astype(jnp.bfloat16)
    fetched = lax.all_to_all(picked, "shard", split_axis=0, concat_axis=0, tiled=True).reshape(
        shards * slots, width
    )
    embedded = fetched[slot]
    vals = embedded.reshape(tok, heads, dval)
    mixed = (
        jnp.einsum("hij,jhd->ihd", weights, vals, preferred_element_type=jnp.float32)
        .reshape(tok, width)
        .astype(jnp.bfloat16)
    )
    back = lax.dot_general(
        cotangent,
        lax.all_gather(out_weight, "shard", axis=0, tiled=True),
        (((1,), (1,)), ((), ())),
        preferred_element_type=jnp.float32,
    ).astype(jnp.bfloat16)
    grad_share = lax.psum_scatter(
        lax.dot_general(
            mixed, cotangent, (((0,), (0,)), ((), ())), preferred_element_type=jnp.float32
        ),
        "shard",
        scatter_dimension=0,
        tiled=True,
    )
    weight_grad = lax.psum(grad_share, "replica").astype(jnp.bfloat16)
    b3 = back.reshape(tok, heads, dval)
    token_grad = jnp.einsum(
        "hij,ihd->jhd", weights, b3, preferred_element_type=jnp.float32
    ).reshape(tok, width)
    send_grad = (
        jnp.zeros((shards * slots, width), jnp.float32)
        .at[slot]
        .set(token_grad)
        .reshape(shards, slots, width)
    )
    arrived = (
        lax.all_to_all(
            send_grad.astype(jnp.bfloat16), "shard", split_axis=0, concat_axis=0, tiled=True
        )
        .astype(send_grad.dtype)
        .reshape(shards * slots, width)
    )
    select = (recv_idx[:, None] == jnp.arange(rows_dev)[None, :]).astype(jnp.float32)
    grad_rows = lax.dot_general(
        select,
        arrived,
        (((0,), (0,)), ((), ())),
        precision=lax.Precision.HIGHEST,
        preferred_element_type=jnp.float32,
    )
    share = lax.psum_scatter(
        grad_rows.astype(jnp.bfloat16), "replica", scatter_dimension=0, tiled=True
    ).astype(jnp.float32)
    quarter = share.shape[0]
    first = lax.axis_index("replica") * quarter
    part_table = lax.dynamic_slice_in_dim(table, first, quarter, 0)
    part_accum = lax.dynamic_slice_in_dim(accum, first, quarter, 0)
    upd_table, upd_accum = adagrad(part_table, part_accum, share)
    new_table, new_accum = (
        lax.all_gather(upd_table, "replica", axis=0, tiled=True),
        lax.all_gather(upd_accum, "replica", axis=0, tiled=True),
    )
    return (new_table, new_accum, weight_grad)


def iota(shape, axis):
    return lax.broadcasted_iota(jnp.int32, shape, axis)


def nt(a, b):
    return lax.dot_general(a, b, (((1,), (1,)), ((), ())), preferred_element_type=F32)


def nn(a, b):
    return lax.dot_general(a, b, (((1,), (0,)), ((), ())), preferred_element_type=F32)


def call(
    kernel,
    name,
    out,
    ins,
    smem=0,
    after=(),
    scratch=(),
    hbm=(),
    limit=16 << 20,
    cost=0,
    placed=False,
    out_hbm=False,
):
    n_in, n_after = len(ins), len(after)
    many = isinstance(out, (list, tuple))

    def run(*refs):
        refs = (*refs[:n_in], *refs[n_in + n_after :])
        if placed:
            shard = lax.axis_index("shard")
            kernel((lax.axis_index("replica"), shard // 2, shard % 2), *refs)
        else:
            kernel(*refs)

    return pl.pallas_call(
        run,
        out_shape=out,
        in_specs=[SMEM if i < smem else HBM if i in hbm else VMEM for i in range(n_in)]
        + [ANY] * n_after,
        out_specs=HBM if out_hbm else [VMEM] * len(out) if many else VMEM,
        scratch_shapes=list(scratch),
        name=name,
        cost_estimate=pl.CostEstimate(flops=cost, bytes_accessed=0, transcendentals=0),
        compiler_params=pltpu.CompilerParams(vmem_limit_bytes=limit),
    )(*ins, *after)


def sds(shape, dtype=BF16):
    return jax.ShapeDtypeStruct(shape, dtype)


def aligned(index, size):
    return pl.ds(pl.multiple_of(index * size, size), size)


def start_all(pairs, sem):
    copies = [pltpu.make_async_copy(a, b, sem.at[i]) for i, (a, b) in enumerate(pairs)]
    for c in copies:
        c.start()
    return copies


def carry_kernel(me, weight, table, out, rows_in, part_in, sem):
    rows, cols = rows_in.shape
    part = part_in.shape[0]
    copies = start_all(
        [
            (table.at[:, aligned(me[0], cols)], rows_in),
            (weight.at[aligned(me[0], part), :], part_in),
        ],
        sem,
    )
    copies[1].wait()
    for i in range((out.shape[0] - rows) // part):
        out[rows + i * part : rows + (i + 1) * part, :] = part_in[:, i * cols : (i + 1) * cols]
    copies[0].wait()
    out[0:rows, :] = rows_in[...].astype(BF16)


def pack_kernel(lens, owner, local, q, k, out, ids, sem):
    n, rows, pw = out.shape
    tok = q.shape[0]
    runs = tok // pw
    later = start_all(
        [
            (x.at[:, i * pw : (i + 1) * pw], out.at[i, j * tok : (j + 1) * tok, :])
            for i in range(n)
            for j, x in enumerate((q, k))
        ],
        sem,
    )
    lane = iota((EXTRA, tok), 1)
    row = iota((EXTRA, tok), 0)
    seg = jnp.zeros((EXTRA, tok), F32)
    end = jnp.int32(0)
    for i in range(lens.shape[1]):
        end = end + lens[0, i]
        seg = seg + jnp.where(lane >= end, 1.0, 0.0)
    all_ids = jnp.where(
        row == 0,
        jnp.broadcast_to(owner[...].astype(F32), (EXTRA, tok)),
        jnp.where(
            row == 1,
            jnp.broadcast_to(local[...].astype(F32), (EXTRA, tok)),
            jnp.where(row == 2, seg, 0.0),
        ),
    ).astype(BF16)
    for i in range(runs):
        ids[i * EXTRA : (i + 1) * EXTRA, :] = all_ids[:, i * pw : (i + 1) * pw]
    later = later + start_all(
        [(ids, out.at[i, 2 * tok : rows, :]) for i in range(n)], sem.at[pl.ds(2 * n, n)]
    )
    for c in later:
        c.wait()


def pass_kernel(x, y, far_y, far_x, sem):
    half = far_x.shape[0]
    copies = start_all([(x.at[half:, :], far_y), (y.at[0:half, :], far_x)], sem)
    for c in copies:
        c.wait()


def stack_kernel(me, *refs):
    *blocks, out = refs
    rows = out.shape[1]
    for m, p in enumerate(blocks):
        out[me[1] ^ m] = p[0:rows, :]


def join_kernel(me, *refs):
    *parts, out = refs
    part = out.shape[0] // len(parts)
    rows = parts[0].shape[1]
    for m, p in enumerate(parts):
        for i in range(p.shape[0] // part):
            out[aligned(me[0] ^ m, part), i * rows : (i + 1) * rows] = p[i * part : (i + 1) * part, :]


def gate_kernel(out):
    out[...] = jnp.zeros_like(out)


def choose_kernel(me, *refs):
    n = (len(refs) - 1) // 2
    parts, out, held = refs[:n], refs[n : 2 * n], refs[2 * n]
    first = parts[0].shape[0] - held.shape[1]
    for m, p in enumerate(parts):
        held[m] = p[first:, :]
    for m, o in enumerate(out):
        o[...] = held[me[1] ^ me[0] ^ m]


def weights_kernel(me, packs, out):
    n, _, pw = packs.shape
    heads, tok = out.shape[1:3]
    dqk = pw // heads
    down, across = iota((tok, tok), 0), iota((tok, tok), 1)
    lane = iota((tok, pw), 1)
    for r in range(n):
        p = packs.at[me[0] ^ r]
        q = p[0:tok, :]
        k = p[tok : 2 * tok, :]
        seg = ids_of(packs, me[0] ^ r, tok)[2:3, :]
        seg_down = jnp.sum(jnp.where(down == across, seg, 0.0), axis=1, keepdims=True)
        mask = (seg == seg_down) & (down <= across)
        for j in range(heads):
            kj = jnp.where(lane // dqk == j, k, jnp.zeros_like(k))
            s = nt(kj, q) * dqk ** (-0.5)
            w = s / (1.0 + jnp.exp(-s)) * (1.0 / MAXLEN)
            out[r, j] = jnp.where(mask, w, 0.0).astype(BF16)


def ids_of(packs, r, tok):
    runs = tok // packs.shape[2]
    ids = packs[r, 2 * tok : 2 * tok + runs * EXTRA, :].astype(F32)
    return jnp.concatenate([ids[i * EXTRA : (i + 1) * EXTRA] for i in range(runs)], axis=1)


def one_hot(ids, shard, rows):
    own, loc = ids[0:1, :], ids[1:2, :]
    named = jnp.where(own == shard.astype(F32), loc, -1.0)
    at = iota((rows, ids.shape[1]), 0).astype(F32)
    return jnp.where(at == named, 1.0, 0.0).astype(BF16)


def mix_kernel(me, packs, w, mine, other, out, picks):
    n, rows, cols = mine.shape
    heads, tok = w.shape[1:3]
    dv = cols // heads
    same = iota((tok, tok), 0) == iota((tok, tok), 1)
    at = iota((tok, rows), 1).astype(F32)
    for r in range(n):
        ids = ids_of(packs, me[0] ^ r, tok)
        own = jnp.sum(jnp.where(same, ids[0:1, :], 0.0), axis=1, keepdims=True)
        loc = jnp.sum(jnp.where(same, ids[1:2, :], 0.0), axis=1, keepdims=True)
        for z in range(n):
            for cc in range(2):
                shard = (2 * z + (me[2] ^ cc)).astype(F32)
                named = jnp.where(own == shard, loc, -1.0)
                first = (2 * z + cc) * rows
                picks[r * tok : (r + 1) * tok, first : first + rows] = jnp.where(
                    at == named, 1.0, 0.0
                ).astype(BF16)
    blocks = jnp.concatenate([x[z] for z in range(n) for x in (mine, other)], axis=0)
    vals = nn(picks[...], blocks).astype(BF16)
    for r in range(n):
        turned = vals[r * tok : (r + 1) * tok, :].T
        for j in range(heads):
            out[j * dv : (j + 1) * dv, r * tok : (r + 1) * tok] = nn(
                turned[j * dv : (j + 1) * dv, :], w[r, j]
            ).astype(BF16)


def by_row(me, packs, grad, core, out):
    n, rows, _ = out.shape
    tok = grad.shape[0] // n
    ids = jnp.concatenate([ids_of(packs, me[0] ^ r, tok) for r in range(n)], axis=1)
    picks = jnp.concatenate([one_hot(ids, 2 * z + core, rows) for z in range(n)], axis=0)
    total = nn(picks, grad[...])
    for z in range(n):
        out[z] = total[z * rows : (z + 1) * rows, :].astype(out.dtype)


def back_kernel(me, packs, ow_mine, ow_other, w, *refs):
    *cots, send, grad, ow = refs
    n = packs.shape[0]
    heads, tok = w.shape[1:3]
    head_rows = ow_mine.shape[0]
    ow[aligned(me[2], head_rows), :] = ow_mine[...]
    ow[aligned(1 - me[2], head_rows), :] = ow_other[...]
    first = 0
    for cot in cots:
        end = first + cot.shape[0]
        grad[first:end, :] = nt(cot[...], ow[...]).astype(BF16)
        first = end
    for r in range(n):
        at_r = slice(r * tok, (r + 1) * tok)
        for j in range(heads):
            at_j = slice(j * head_rows, (j + 1) * head_rows)
            grad[at_r, at_j] = nn(w[r, j], grad[at_r, at_j]).astype(BF16)
    by_row(me, packs, grad, 1 - me[2], send)


def keep_kernel(me, packs, grad, keep):
    by_row(me, packs, grad, me[2], keep)


def wgrad_kernel(me, mixed, *refs):
    *cots, keep, send = refs
    rows = keep.shape[0]
    for cc, out in ((1, send), (0, keep)):
        at = aligned(me[2] ^ cc, rows)
        total = jnp.zeros(keep.shape, F32)
        first = 0
        for cot in cots:
            end = first + cot.shape[0]
            total = total + nn(mixed[at, first:end], cot[...])
            first = end
        out[...] = total.astype(out.dtype)


def add_kernel(keep, got, out):
    out[...] = (keep[...] + got[...].astype(F32)).astype(out.dtype)


def add_parts_kernel(me, keep, got, *out):
    rows = out[0].shape[0]
    for m, o in enumerate(out):
        at = aligned(me[0] ^ m, rows)
        o[...] = (keep[at, :] + got[at, :].astype(F32)).astype(o.dtype)


def sum_first_kernel(parts, out):
    total = parts[0].astype(F32)
    for m in range(1, parts.shape[0]):
        total = total + parts[m].astype(F32)
    out[...] = total.astype(out.dtype)


def sum_kernel(*refs):
    *parts, out = refs
    total = parts[0][...].astype(F32)
    for p in parts[1:]:
        total = total + p[...].astype(F32)
    out[...] = total.astype(out.dtype)


def place_kernel(me, *refs):
    *parts, out = refs
    rows = parts[0].shape[0]
    for m, p in enumerate(parts):
        out[aligned(me[0] ^ m, rows), :] = p[...]


def update_kernel(me, table, accum, *refs):
    *parts, new_table, new_accum, grad = refs
    rows, width = table.shape
    cols = width // len(parts)
    for m, p in enumerate(parts):
        grad[:, aligned(me[0] ^ m, cols)] = p[...]
    g = grad[...].astype(F32)
    mean = jnp.sum(g * g, axis=1, keepdims=True) * (1.0 / width)
    same = iota((rows, rows), 0) == iota((rows, rows), 1)
    old = jnp.sum(jnp.where(same, accum[...], 0.0), axis=1, keepdims=True)
    fresh = old + mean
    new_accum[...] = jnp.sum(jnp.where(same, fresh, 0.0), axis=0, keepdims=True)
    new_table[...] = table[...] - g / (jnp.sqrt(fresh) + 1e-08)


def body(table, accum, owner, local_row, lengths, queries, keys, cotangent, out_weight):
    n = lax.axis_size("replica")
    shards = lax.axis_size("shard")
    tok = owner.shape[0]
    rows, width = table.shape
    cols = width // n
    heads = HEADS // n
    part = out_weight.shape[0] // n

    def column(x, m):
        return lax.ppermute(x, "replica", [(i, i ^ m) for i in range(n)]) if m else x

    def along(x, m):
        return lax.ppermute(x, "shard", [(i, i ^ (2 * m)) for i in range(shards)]) if m else x

    def core(x):
        return lax.ppermute(x, "shard", [(i, i ^ 1) for i in range(shards)])

    def swap_along(x):
        groups = [list(range(c, shards, 2)) for c in range(2)]
        return lax.all_to_all(x, "shard", 0, 0, tiled=True, axis_index_groups=groups)

    def swap_columns(x):
        return lax.all_to_all(x, "replica", 0, 0, tiled=True)

    half = tok // 2
    x, y = column(cotangent, 1), column(cotangent, 2)
    zrows = rows + part * width // cols
    zpay = call(
        carry_kernel,
        "carry",
        sds((zrows, cols)),
        (out_weight, table),
        hbm=(0, 1),
        scratch=[
            pltpu.VMEM((rows, cols), F32),
            pltpu.VMEM((part, width), BF16),
            pltpu.SemaphoreType.DMA((2,)),
        ],
        limit=None,
        placed=True,
    )
    pw = queries.shape[1] // n
    packs = call(
        pack_kernel,
        "pack",
        sds((n, 2 * tok + tok // pw * EXTRA, pw)),
        (lengths, owner.reshape(1, tok), local_row.reshape(1, tok), queries, keys),
        smem=1,
        out_hbm=True,
        scratch=[
            pltpu.VMEM((tok // pw * EXTRA, pw), BF16),
            pltpu.SemaphoreType.DMA((3 * n,)),
        ],
    )
    packs = swap_columns(packs)
    blocks = [along(zpay, m) for m in range(n)]
    far_y, far_x = call(
        pass_kernel,
        "pass",
        [sds((half, width))] * 2,
        (x, y),
        scratch=[pltpu.SemaphoreType.DMA((2,))],
        cost=PASS_COST,
    )
    w = call(
        weights_kernel,
        "weights",
        sds((n, heads, tok, tok)),
        (packs,),
        after=(far_x,),
        placed=True,
    )
    owp = call(
        choose_kernel,
        "choose",
        [sds((zrows - rows, cols))] * n,
        blocks,
        after=(packs,),
        scratch=[pltpu.VMEM((n, zrows - rows, cols), BF16)],
        placed=True,
    )
    mine = call(
        stack_kernel, "stack", sds((n, rows, cols)), blocks, after=(owp[0],), placed=True
    )
    other = core(mine)
    owp = [column(p, m) for m, p in enumerate(owp)]
    ow_mine = call(join_kernel, "join", sds((n * part, width)), owp, placed=True)
    ow_other = core(ow_mine)
    far_y, far_x = column(far_y, 2), column(far_x, 1)
    cots = [cotangent, x, y, far_x, far_y]
    here = call(gate_kernel, "gate", sds((8, 128), F32), (), after=(far_x, far_y), cost=GATE_COST)

    mixed = call(
        mix_kernel,
        "mix",
        sds((cols, n * tok)),
        (packs, w, mine, other),
        scratch=[pltpu.VMEM((n * tok, shards * rows), BF16)],
        placed=True,
    )
    send, grad = call(
        back_kernel,
        "back",
        [sds((n, rows, cols)), sds((n * tok, cols))],
        (packs, ow_mine, ow_other, w, *cots),
        after=(here, mixed),
        scratch=[pltpu.VMEM((cols, width), BF16)],
        placed=True,
    )
    got = core(send)
    keep = call(keep_kernel, "keep", sds((n, rows, cols), F32), (packs, grad), placed=True)
    sums = call(add_kernel, "add", sds((n, rows, cols)), (keep, got))
    ready = sums
    sums = swap_along(sums)
    wkeep, wsend = call(
        wgrad_kernel,
        "wgrad",
        [sds((n * part, width), F32), sds((n * part, width))],
        (mixed, *cots),
        after=(ready,),
        placed=True,
    )
    wgot = core(wsend)

    wparts = call(
        add_parts_kernel, "add_parts", [sds((part, width))] * n, (wkeep, wgot), placed=True
    )
    wparts = [column(p, m) for m, p in enumerate(wparts)]
    wparts = call(
        choose_kernel,
        "pick",
        [sds((part, width))] * n,
        wparts,
        placed=True,
        scratch=[pltpu.VMEM((n, part, width), BF16)],
    )
    wparts = [along(p, m) for m, p in enumerate(wparts)]

    grad = call(sum_first_kernel, "sum_rows", sds((rows, cols)), (sums,))
    grads = [column(grad, m) for m in range(n)]
    there = call(
        gate_kernel,
        "gate_parts",
        sds((8, 128), F32),
        (),
        after=tuple(wparts[1:]),
        cost=PARTS_COST,
    )
    wsum = call(sum_kernel, "sum_parts", sds((part, width)), wparts, after=(grad, there))
    wsums = [column(wsum, m) for m in range(n)]
    new_table, new_accum = call(
        update_kernel,
        "update",
        [sds((rows, width), F32), sds((1, rows), F32)],
        (table, accum.reshape(1, rows), *grads),
        cost=UPDATE_COST,
        placed=True,
        scratch=[pltpu.VMEM((rows, width), BF16)],
    )
    weight_grad = call(
        place_kernel, "place", sds((n * part, width)), wsums, after=(new_accum,), placed=True
    )
    return (new_table, new_accum.reshape(rows), weight_grad)


def fits(mesh):
    n, shards = mesh.shape["replica"], mesh.shape["shard"]
    return n & (n - 1) == 0 and shards == HEADS and 2 * n == HEADS


def solution(mesh):
    placed = (
        P("shard", None),
        P("shard"),
        P(("replica", "shard"), None),
        P(("replica", "shard")),
        P(("replica", "shard"), None),
        P(("replica", "shard"), None),
        P(("replica", "shard"), None),
        P(("replica", "shard"), None),
        P("shard", None),
    )
    return jax.shard_map(
        body if fits(mesh) else general_body,
        mesh=mesh,
        in_specs=placed,
        out_specs=(P("shard", None), P("shard"), P("shard", None)),
        check_vma=False,
    )
```
